32 devices in a mesh: ctx: 8 (over z, y), tp: 4 (over x, core).
Axes of the slice: x: 2, y: 2, z: 4, core: 2. Of those that a mesh axis runs over, the one named last changes fastest.
Arguments:
- streams: bfloat16 [3, 256, 1024], P(None, 'tp', 'ctx'), may hold values from -6 to 6
- filter_raw: float32 [256, 1024], P('tp', 'ctx'), may hold values from -6 to 6
- grad_output: bfloat16 [256, 1024], P('tp', 'ctx'), may hold values from -6 to 6
Outputs:
- mixed_out: bfloat16 [256, 1024], P('tp', 'ctx')
- grad_streams: bfloat16 [3, 256, 1024], P(None, 'tp', 'ctx')
- grad_filter: float32 [256, 1024], P('tp', 'ctx')
The draws below stay inside these ranges and needn't reach their ends.
All inputs are finite; a program needn't handle non-finite values.
Results may differ from the reference program's by a relative error of at most 0.0014.
Values sent between devices are 32-bit elements; how exact they have to be, the bound alone decides.
No kernel may reach another device: no remote copies, remote signals or barrier semaphores. Data moves between devices by JAX's collectives and lax.ppermute only.
A program may use at most 64 MiB of HBM per device.

```python
import jax
import jax.numpy as jnp

SLAB = 256
TOKENS = 1024


def level_of(rng, dims, pieces, low, largest):
    def one(axis_at, shards_of):
        heights = jax.random.uniform(jax.random.fold_in(jax.random.fold_in(rng, 6), axis_at), (shards_of,), jnp.float32, low / len(pieces), largest / len(pieces))
        return jnp.repeat(jnp.exp(heights), dims[axis_at] // shards_of).reshape((-1,) + (1,) * (len(dims) - axis_at - 1))

    level = one(*pieces[0])
    for cut in pieces[1:]:
        level = level * one(*cut)
    return level


def scatter_about(own_key, extent, width, reach, cuts=(), kind=jnp.bfloat16):
    values = jax.random.normal(own_key, extent, jnp.float32) * width
    if len(cuts) > 0:
        values = level_of(own_key, extent, cuts, -0.22, 0.18) * values
    return jnp.clip(values, min=-reach, max=reach).astype(kind)


def setup_inputs(seed: int = 0) -> dict:
    streams_of = jax.random.split(jax.random.key(seed), 4)
    streams = scatter_about(streams_of[0], (3, SLAB, TOKENS), 1.0, 6.0, ((1, 4), (2, 8)))
    filter_raw = scatter_about(streams_of[1], (SLAB, TOKENS), 1.0, 6.0, ((0, 4), (1, 8)), jnp.float32)
    grad_output = scatter_about(streams_of[2], (SLAB, TOKENS), 1.0, 6.0, ((0, 4), (1, 8)))
    return {"streams": streams, "filter_raw": filter_raw, "grad_output": grad_output}


def reference(streams, filter_raw, grad_output):
    query_part = streams[0].astype(jnp.float32)
    key_part = streams[1].astype(jnp.float32)
    value_part = streams[2].astype(jnp.float32)
    gated_input = key_part * value_part
    tap_scale = 1.0 / TOKENS ** 0.5
    kernel_taps = filter_raw.astype(jnp.float32) * tap_scale
    length = 2 * TOKENS
    spec_gated = jnp.fft.rfft(gated_input, n=length, axis=1)
    spec_taps = jnp.fft.rfft(kernel_taps, n=length, axis=1)
    long_conv = jnp.fft.irfft(spec_gated * spec_taps, n=length, axis=1)[:, :TOKENS]
    mixed_out = (query_part * long_conv).astype(jnp.bfloat16)
    upstream = grad_output.astype(jnp.float32)
    grad_conv = query_part * upstream
    grad_query = (upstream * long_conv).astype(jnp.bfloat16)
    spec_grad = jnp.fft.rfft(grad_conv, n=length, axis=1)
    grad_gated = jnp.fft.irfft(spec_grad * jnp.conj(spec_taps), n=length, axis=1)[:, :TOKENS]
    grad_filter = jnp.fft.irfft(spec_grad * jnp.conj(spec_gated), n=length, axis=1)[:, :TOKENS] * tap_scale
    grad_key = (grad_gated * value_part).astype(jnp.bfloat16)
    grad_value = (grad_gated * key_part).astype(jnp.bfloat16)
    grad_streams = jnp.stack([grad_query, grad_key, grad_value], axis=0)
    return mixed_out, grad_streams, grad_filter.astype(jnp.float32)
```

```python
import math

import jax
import jax.numpy as jnp
import numpy as np
from jax import lax
from jax.experimental import pallas as pl
from jax.experimental.pallas import tpu as pltpu
from jax.sharding import PartitionSpec as P

highest = lax.Precision.HIGHEST


def dft_tables(slow, fast, devices, position):
    length = slow * fast
    stride = fast // devices
    freq_slow = jnp.arange(slow, dtype=jnp.int32)
    rows_slow = jnp.arange(devices, dtype=jnp.int32)
    angle_slow = (
        2.0 * math.pi / slow * (freq_slow[:, None] * rows_slow[None, :] % slow).astype(jnp.float32)
    )
    cols_twist = position * stride + jnp.arange(stride, dtype=jnp.int32)
    angle_twist = (
        2.0
        * math.pi
        / length
        * (freq_slow[:, None] * cols_twist[None, :] % length).astype(jnp.float32)
    )
    freq_fast = jnp.arange(fast, dtype=jnp.int32)
    angle_fast = (
        2.0 * math.pi / fast * (freq_fast[:, None] * freq_fast[None, :] % fast).astype(jnp.float32)
    )
    return (
        jnp.cos(angle_slow),
        jnp.sin(angle_slow),
        jnp.cos(angle_twist)[:, None, :],
        jnp.sin(angle_twist)[:, None, :],
        jnp.cos(angle_fast),
        jnp.sin(angle_fast),
    )


def forward_spectrum(signal, tables):
    cos_slow, sin_slow, cos_twist, sin_twist, cos_fast, sin_fast = tables
    stacked, channels, fast = signal.shape
    slow, devices = cos_slow.shape
    stride = fast // devices
    columns = lax.all_to_all(signal[:, None], "ctx", split_axis=3, concat_axis=1, tiled=True)
    flat = columns.reshape(stacked, devices, channels * stride)
    real_part = jnp.einsum("ka,sam->skm", cos_slow, flat, precision=highest).reshape(
        stacked, slow, channels, stride
    )
    imag_part = -jnp.einsum("ka,sam->skm", sin_slow, flat, precision=highest).reshape(
        stacked, slow, channels, stride
    )
    turned_real = real_part * cos_twist + imag_part * sin_twist
    turned_imag = imag_part * cos_twist - real_part * sin_twist
    rows_real, rows_imag = (
        lax.all_to_all(turned_real, "ctx", split_axis=1, concat_axis=3, tiled=True),
        lax.all_to_all(turned_imag, "ctx", split_axis=1, concat_axis=3, tiled=True),
    )
    spec_real = jnp.matmul(rows_real, cos_fast, precision=highest) + jnp.matmul(
        rows_imag, sin_fast, precision=highest
    )
    spec_imag = jnp.matmul(rows_imag, cos_fast, precision=highest) - jnp.matmul(
        rows_real, sin_fast, precision=highest
    )
    return (spec_real, spec_imag)


def inverse_signal(spec_real, spec_imag, tables):
    cos_slow, sin_slow, cos_twist, sin_twist, cos_fast, sin_fast = tables
    stacked, local_rows, channels, fast = spec_real.shape
    slow, devices = cos_slow.shape
    stride = fast // devices
    back_real = jnp.matmul(spec_real, cos_fast, precision=highest) - jnp.matmul(
        spec_imag, sin_fast, precision=highest
    )
    back_imag = jnp.matmul(spec_imag, cos_fast, precision=highest) + jnp.matmul(
        spec_real, sin_fast, precision=highest
    )
    cols_real, cols_imag = (
        lax.all_to_all(back_real, "ctx", split_axis=3, concat_axis=1, tiled=True),
        lax.all_to_all(back_imag, "ctx", split_axis=3, concat_axis=1, tiled=True),
    )
    turned_real = (cols_real * cos_twist - cols_imag * sin_twist).reshape(
        stacked, slow, channels * stride
    )
    turned_imag = (cols_imag * cos_twist + cols_real * sin_twist).reshape(
        stacked, slow, channels * stride
    )
    timeline = jnp.einsum("ka,skm->sam", cos_slow, turned_real, precision=highest) - jnp.einsum(
        "ka,skm->sam", sin_slow, turned_imag, precision=highest
    )
    timeline = timeline.reshape(stacked, devices, channels, stride)
    returned = lax.all_to_all(timeline, "ctx", split_axis=1, concat_axis=3, tiled=True)
    return returned[:, 0] / float(slow * fast)


def conv_product(gated_real, gated_imag, taps_real, taps_imag):
    conv_real = gated_real * taps_real - gated_imag * taps_imag
    conv_imag = gated_real * taps_imag + gated_imag * taps_real
    return (conv_real, conv_imag)


def corr_products(grad_real, grad_imag, gated_real, gated_imag, taps_real, taps_imag):
    corr_real = jnp.stack(
        [
            grad_real * taps_real + grad_imag * taps_imag,
            grad_real * gated_real + grad_imag * gated_imag,
        ]
    )
    corr_imag = jnp.stack(
        [
            grad_imag * taps_real - grad_real * taps_imag,
            grad_imag * gated_real - grad_real * gated_imag,
        ]
    )
    return (corr_real, corr_imag)


def by_residue(streams, filter_raw, grad_output):
    devices = lax.axis_size("ctx")
    position = lax.axis_index("ctx")
    channels, fast = filter_raw.shape
    slow = 2 * devices
    tap_scale = 1.0 / math.sqrt(fast * devices)
    tables = dft_tables(slow, fast, devices, position)
    query_part = streams[0].astype(jnp.float32)
    key_part = streams[1].astype(jnp.float32)
    value_part = streams[2].astype(jnp.float32)
    gated_input = key_part * value_part
    kernel_taps = filter_raw * tap_scale
    upstream = grad_output.astype(jnp.float32)
    grad_conv = query_part * upstream
    spec_real, spec_imag = forward_spectrum(jnp.stack([gated_input, kernel_taps]), tables)
    conv_real, conv_imag = conv_product(spec_real[0], spec_imag[0], spec_real[1], spec_imag[1])
    long_conv = inverse_signal(conv_real[None], conv_imag[None], tables)[0]
    grad_real, grad_imag = forward_spectrum(grad_conv[None], tables)
    corr_real, corr_imag = corr_products(
        grad_real[0], grad_imag[0], spec_real[0], spec_imag[0], spec_real[1], spec_imag[1]
    )
    both_back = inverse_signal(corr_real, corr_imag, tables)
    grad_gated = both_back[0]
    filter_back = both_back[1]
    grad_filter = filter_back * tap_scale
    mixed_out = (query_part * long_conv).astype(jnp.bfloat16)
    grad_query = (upstream * long_conv).astype(jnp.bfloat16)
    grad_key = (grad_gated * value_part).astype(jnp.bfloat16)
    grad_value = (grad_gated * key_part).astype(jnp.bfloat16)
    grad_streams = jnp.stack([grad_query, grad_key, grad_value], axis=0)
    return (mixed_out, grad_streams, grad_filter)


def table(angle):
    return np.cos(angle), np.sin(angle)


def circle(count, at):
    exact = {0: (1.0, 0.0), 1: (0.0, 1.0), 2: (-1.0, 0.0), 3: (0.0, -1.0)}
    at = at % count
    if 4 * at % count == 0:
        return exact[4 * at // count]
    return math.cos(2.0 * math.pi * at / count), math.sin(2.0 * math.pi * at / count)


def weighted(terms):
    total = None
    for weight, array in terms:
        if weight == 0.0 or array is None:
            continue
        if total is None:
            total = array if weight == 1.0 else -array if weight == -1.0 else array * weight
        elif weight == 1.0:
            total = total + array
        elif weight == -1.0:
            total = total - array
        else:
            total = total + array * weight
    return total


def transform_tables(devices, fast, scale):
    slow = 2 * devices
    length = slow * fast
    at = np.arange(fast)
    cos, sin = table(2.0 * np.pi / fast * (at[:, None] * at[None, :] % fast))
    matrix = np.block([[cos, -sin], [sin, cos]]).astype(np.float32)
    high = matrix.astype(jnp.bfloat16)
    low = (matrix - high.astype(np.float32)).astype(jnp.bfloat16)
    rows = np.arange(devices + 1)
    cos, sin = table(2.0 * np.pi / length * (rows[:, None] * at[None, :] % length))
    weight = np.where((rows == 0) | (rows == devices), 1.0, 2.0)[:, None] * scale / length
    turns = np.concatenate([cos, sin, cos * weight, sin * weight]).astype(np.float32)
    return high, low, turns


def product(left, high, low):
    left_high = left.astype(jnp.bfloat16)
    left_low = (left - left_high.astype(jnp.float32)).astype(jnp.bfloat16)

    def dot(a, b):
        return jnp.dot(a, b, preferred_element_type=jnp.float32)

    return dot(left_high, high) + (dot(left_low, high) + dot(left_high, low))


def gate_kernel(streams_ref, filter_ref, upstream_ref, out_ref):
    devices, stacked, fast = out_ref.shape
    group = stacked // 3
    query_part = streams_ref[0].astype(jnp.float32)
    key_part = streams_ref[1].astype(jnp.float32)
    value_part = streams_ref[2].astype(jnp.float32)
    upstream = upstream_ref[...].astype(jnp.float32)
    out_ref[:, :group] = (key_part * value_part).reshape(devices, group, fast)
    out_ref[:, group : 2 * group] = filter_ref[...].reshape(devices, group, fast)
    out_ref[:, 2 * group :] = (query_part * upstream).reshape(devices, group, fast)


def convolve_kernel(signal_ref, high_ref, low_ref, turns_ref, out_ref):
    devices, stacked, fast = signal_ref.shape
    slow, group = 2 * devices, stacked // 3
    count = devices + 1

    def turn(which, k):
        return turns_ref[which * count + k : which * count + k + 1, :]

    signal = [signal_ref[a] for a in range(devices)]
    real, imag = [None] * count, [None] * count
    for k in range(devices // 2 + 1):
        sums = [
            weighted([(circle(slow, a * k)[part], signal[a]) for a in range(parity, devices, 2)])
            for part in range(2)
            for parity in range(2)
        ]
        cos_even, cos_odd, sin_even, sin_odd = sums
        real[k] = weighted([(1.0, cos_even), (1.0, cos_odd)])
        imag[k] = weighted([(-1.0, sin_even), (-1.0, sin_odd)])
        if 2 * k != devices:
            real[devices - k] = weighted([(1.0, cos_even), (-1.0, cos_odd)])
            imag[devices - k] = weighted([(1.0, sin_even), (-1.0, sin_odd)])
    rows = []
    for k in range(count):
        cos, sin = turn(0, k), turn(1, k)
        if k == 0:
            turned = (real[k], jnp.zeros_like(real[k]))
        elif imag[k] is None:
            turned = (real[k] * cos, -(real[k] * sin))
        else:
            turned = (real[k] * cos + imag[k] * sin, imag[k] * cos - real[k] * sin)
        rows.append(jnp.concatenate(turned, axis=1))
    high, low = high_ref[...], low_ref[...]
    spectrum = product(jnp.concatenate(rows, axis=0), high, low)
    rows = []
    for k in range(count):
        base = k * stacked
        parts = [spectrum[base + i * group : base + (i + 1) * group] for i in range(3)]
        (gated_real, taps_real, grad_real) = (p[:, :fast] for p in parts)
        (gated_imag, taps_imag, grad_imag) = (p[:, fast:] for p in parts)
        rows.append(
            jnp.concatenate(
                [
                    jnp.concatenate(
                        [
                            gated_real * taps_real - gated_imag * taps_imag,
                            -(gated_real * taps_imag + gated_imag * taps_real),
                        ],
                        axis=1,
                    ),
                    jnp.concatenate(
                        [
                            grad_real * taps_real + grad_imag * taps_imag,
                            grad_real * taps_imag - grad_imag * taps_real,
                        ],
                        axis=1,
                    ),
                    jnp.concatenate(
                        [
                            grad_real * gated_real + grad_imag * gated_imag,
                            grad_real * gated_imag - grad_imag * gated_real,
                        ],
                        axis=1,
                    ),
                ],
                axis=0,
            )
        )
    back = product(jnp.concatenate(rows, axis=0), high, low)
    real, imag = [], []
    for k in range(count):
        cos, sin = turn(2, k), turn(3, k)
        row = back[k * stacked : (k + 1) * stacked]
        real.append(row[:, :fast] * cos + row[:, fast:] * sin)
        imag.append(row[:, fast:] * cos - row[:, :fast] * sin)
    half = devices // 2
    for parity in range(2):
        sign = 1.0 - 2.0 * parity
        cos_part = [weighted([(1.0, real[k]), (sign, real[devices - k])]) for k in range(half)]
        sin_part = [weighted([(1.0, imag[k]), (-sign, imag[devices - k])]) for k in range(half)]
        for a in range(parity, devices, 2):
            terms = [(circle(slow, a * k)[0], cos_part[k]) for k in range(half)]
            terms += [(circle(slow, a * k)[1], sin_part[k]) for k in range(1, half)]
            terms += [(circle(slow, a * half)[0], real[half]), (circle(slow, a * half)[1], imag[half])]
            out_ref[a] = weighted(terms)


def output_kernel(back_ref, streams_ref, upstream_ref, mixed_ref, streams_grad_ref, filter_grad_ref):
    channels, fast = filter_grad_ref.shape
    group = back_ref.shape[1] // 3
    long_conv = back_ref[:, :group].reshape(channels, fast)
    grad_gated = back_ref[:, group : 2 * group].reshape(channels, fast)
    filter_grad_ref[...] = back_ref[:, 2 * group :].reshape(channels, fast)
    mixed_ref[...] = (streams_ref[0].astype(jnp.float32) * long_conv).astype(jnp.bfloat16)
    streams_grad_ref[0] = (upstream_ref[...].astype(jnp.float32) * long_conv).astype(jnp.bfloat16)
    streams_grad_ref[1] = (streams_ref[2].astype(jnp.float32) * grad_gated).astype(jnp.bfloat16)
    streams_grad_ref[2] = (streams_ref[1].astype(jnp.float32) * grad_gated).astype(jnp.bfloat16)


def by_channel(streams, filter_raw, grad_output):
    devices = lax.axis_size("ctx")
    channels, fast = filter_raw.shape
    stacked = 3 * (channels // devices)
    tap_scale = 1.0 / math.sqrt(fast * devices)
    vmem = pl.BlockSpec(memory_space=pltpu.VMEM)
    regrouped = jax.ShapeDtypeStruct((devices, stacked, fast), jnp.float32)
    signals = pl.pallas_call(gate_kernel, out_shape=regrouped, in_specs=[vmem] * 3, out_specs=vmem)(
        streams, filter_raw, grad_output
    )
    signals = lax.all_to_all(signals, "ctx", split_axis=0, concat_axis=0, tiled=True)
    tables = transform_tables(devices, fast, tap_scale)
    results = pl.pallas_call(convolve_kernel, out_shape=regrouped, in_specs=[vmem] * 4, out_specs=vmem)(
        signals, *tables
    )
    results = lax.all_to_all(results, "ctx", split_axis=0, concat_axis=0, tiled=True)
    return pl.pallas_call(
        output_kernel,
        out_shape=(
            jax.ShapeDtypeStruct((channels, fast), jnp.bfloat16),
            jax.ShapeDtypeStruct((3, channels, fast), jnp.bfloat16),
            jax.ShapeDtypeStruct((channels, fast), jnp.float32),
        ),
        in_specs=[vmem] * 3,
        out_specs=(vmem,) * 3,
    )(results, streams, grad_output)


def local(streams, filter_raw, grad_output):
    devices = lax.axis_size("ctx")
    channels, fast = filter_raw.shape
    if devices % 2 == 0 and channels % (8 * devices) == 0 and fast % 128 == 0:
        return by_channel(streams, filter_raw, grad_output)
    return by_residue(streams, filter_raw, grad_output)


def solution(mesh):
    in_specs = (P(None, "tp", "ctx"), P("tp", "ctx"), P("tp", "ctx"))
    out_specs = (P("tp", "ctx"), P(None, "tp", "ctx"), P("tp", "ctx"))
    return jax.shard_map(local, mesh=mesh, in_specs=in_specs, out_specs=out_specs, check_vma=False)
```

```python
import math

import jax
import jax.numpy as jnp
import numpy as np
from jax import lax
from jax.experimental import pallas as pl
from jax.experimental.pallas import tpu as pltpu
from jax.sharding import PartitionSpec as P

highest = lax.Precision.HIGHEST


def dft_tables(slow, fast, devices, position):
    length = slow * fast
    stride = fast // devices
    freq_slow = jnp.arange(slow, dtype=jnp.int32)
    rows_slow = jnp.arange(devices, dtype=jnp.int32)
    angle_slow = (
        2.0 * math.pi / slow * (freq_slow[:, None] * rows_slow[None, :] % slow).astype(jnp.float32)
    )
    cols_twist = position * stride + jnp.arange(stride, dtype=jnp.int32)
    angle_twist = (
        2.0
        * math.pi
        / length
        * (freq_slow[:, None] * cols_twist[None, :] % length).astype(jnp.float32)
    )
    freq_fast = jnp.arange(fast, dtype=jnp.int32)
    angle_fast = (
        2.0 * math.pi / fast * (freq_fast[:, None] * freq_fast[None, :] % fast).astype(jnp.float32)
    )
    return (
        jnp.cos(angle_slow),
        jnp.sin(angle_slow),
        jnp.cos(angle_twist)[:, None, :],
        jnp.sin(angle_twist)[:, None, :],
        jnp.cos(angle_fast),
        jnp.sin(angle_fast),
    )


def forward_spectrum(signal, tables):
    cos_slow, sin_slow, cos_twist, sin_twist, cos_fast, sin_fast = tables
    stacked, channels, fast = signal.shape
    slow, devices = cos_slow.shape
    stride = fast // devices
    columns = lax.all_to_all(signal[:, None], "ctx", split_axis=3, concat_axis=1, tiled=True)
    flat = columns.reshape(stacked, devices, channels * stride)
    real_part = jnp.einsum("ka,sam->skm", cos_slow, flat, precision=highest).reshape(
        stacked, slow, channels, stride
    )
    imag_part = -jnp.einsum("ka,sam->skm", sin_slow, flat, precision=highest).reshape(
        stacked, slow, channels, stride
    )
    turned_real = real_part * cos_twist + imag_part * sin_twist
    turned_imag = imag_part * cos_twist - real_part * sin_twist
    rows_real, rows_imag = (
        lax.all_to_all(turned_real, "ctx", split_axis=1, concat_axis=3, tiled=True),
        lax.all_to_all(turned_imag, "ctx", split_axis=1, concat_axis=3, tiled=True),
    )
    spec_real = jnp.matmul(rows_real, cos_fast, precision=highest) + jnp.matmul(
        rows_imag, sin_fast, precision=highest
    )
    spec_imag = jnp.matmul(rows_imag, cos_fast, precision=highest) - jnp.matmul(
        rows_real, sin_fast, precision=highest
    )
    return (spec_real, spec_imag)


def inverse_signal(spec_real, spec_imag, tables):
    cos_slow, sin_slow, cos_twist, sin_twist, cos_fast, sin_fast = tables
    stacked, local_rows, channels, fast = spec_real.shape
    slow, devices = cos_slow.shape
    stride = fast // devices
    back_real = jnp.matmul(spec_real, cos_fast, precision=highest) - jnp.matmul(
        spec_imag, sin_fast, precision=highest
    )
    back_imag = jnp.matmul(spec_imag, cos_fast, precision=highest) + jnp.matmul(
        spec_real, sin_fast, precision=highest
    )
    cols_real, cols_imag = (
        lax.all_to_all(back_real, "ctx", split_axis=3, concat_axis=1, tiled=True),
        lax.all_to_all(back_imag, "ctx", split_axis=3, concat_axis=1, tiled=True),
    )
    turned_real = (cols_real * cos_twist - cols_imag * sin_twist).reshape(
        stacked, slow, channels * stride
    )
    turned_imag = (cols_imag * cos_twist + cols_real * sin_twist).reshape(
        stacked, slow, channels * stride
    )
    timeline = jnp.einsum("ka,skm->sam", cos_slow, turned_real, precision=highest) - jnp.einsum(
        "ka,skm->sam", sin_slow, turned_imag, precision=highest
    )
    timeline = timeline.reshape(stacked, devices, channels, stride)
    returned = lax.all_to_all(timeline, "ctx", split_axis=1, concat_axis=3, tiled=True)
    return returned[:, 0] / float(slow * fast)


def conv_product(gated_real, gated_imag, taps_real, taps_imag):
    conv_real = gated_real * taps_real - gated_imag * taps_imag
    conv_imag = gated_real * taps_imag + gated_imag * taps_real
    return (conv_real, conv_imag)


def corr_products(grad_real, grad_imag, gated_real, gated_imag, taps_real, taps_imag):
    corr_real = jnp.stack(
        [
            grad_real * taps_real + grad_imag * taps_imag,
            grad_real * gated_real + grad_imag * gated_imag,
        ]
    )
    corr_imag = jnp.stack(
        [
            grad_imag * taps_real - grad_real * taps_imag,
            grad_imag * gated_real - grad_real * gated_imag,
        ]
    )
    return (corr_real, corr_imag)


def by_residue(streams, filter_raw, grad_output):
    devices = lax.axis_size("ctx")
    position = lax.axis_index("ctx")
    channels, fast = filter_raw.shape
    slow = 2 * devices
    tap_scale = 1.0 / math.sqrt(fast * devices)
    tables = dft_tables(slow, fast, devices, position)
    query_part = streams[0].astype(jnp.float32)
    key_part = streams[1].astype(jnp.float32)
    value_part = streams[2].astype(jnp.float32)
    gated_input = key_part * value_part
    kernel_taps = filter_raw * tap_scale
    upstream = grad_output.astype(jnp.float32)
    grad_conv = query_part * upstream
    spec_real, spec_imag = forward_spectrum(jnp.stack([gated_input, kernel_taps]), tables)
    conv_real, conv_imag = conv_product(spec_real[0], spec_imag[0], spec_real[1], spec_imag[1])
    long_conv = inverse_signal(conv_real[None], conv_imag[None], tables)[0]
    grad_real, grad_imag = forward_spectrum(grad_conv[None], tables)
    corr_real, corr_imag = corr_products(
        grad_real[0], grad_imag[0], spec_real[0], spec_imag[0], spec_real[1], spec_imag[1]
    )
    both_back = inverse_signal(corr_real, corr_imag, tables)
    grad_gated = both_back[0]
    filter_back = both_back[1]
    grad_filter = filter_back * tap_scale
    mixed_out = (query_part * long_conv).astype(jnp.bfloat16)
    grad_query = (upstream * long_conv).astype(jnp.bfloat16)
    grad_key = (grad_gated * value_part).astype(jnp.bfloat16)
    grad_value = (grad_gated * key_part).astype(jnp.bfloat16)
    grad_streams = jnp.stack([grad_query, grad_key, grad_value], axis=0)
    return (mixed_out, grad_streams, grad_filter)


def table(angle):
    return np.cos(angle), np.sin(angle)


def circle(count, at):
    exact = {0: (1.0, 0.0), 1: (0.0, 1.0), 2: (-1.0, 0.0), 3: (0.0, -1.0)}
    at = at % count
    if 4 * at % count == 0:
        return exact[4 * at // count]
    return math.cos(2.0 * math.pi * at / count), math.sin(2.0 * math.pi * at / count)


def weighted(terms):
    total = None
    for weight, array in terms:
        if weight == 0.0 or array is None:
            continue
        if total is None:
            total = array if weight == 1.0 else -array if weight == -1.0 else array * weight
        elif weight == 1.0:
            total = total + array
        elif weight == -1.0:
            total = total - array
        else:
            total = total + array * weight
    return total


def transform_tables(devices, fast, scale):
    slow = 2 * devices
    length = slow * fast
    at = np.arange(fast)
    cos, sin = table(2.0 * np.pi / fast * (at[:, None] * at[None, :] % fast))
    matrix = np.block([[cos, -sin], [sin, cos]]).astype(np.float32)
    high = matrix.astype(jnp.bfloat16)
    low = (matrix - high.astype(np.float32)).astype(jnp.bfloat16)
    rows = np.arange(devices + 1)
    cos, sin = table(2.0 * np.pi / length * (rows[:, None] * at[None, :] % length))
    weight = np.where((rows == 0) | (rows == devices), 1.0, 2.0)[:, None] * scale / length
    turns = np.concatenate([cos, sin, cos * weight, sin * weight]).astype(np.float32)
    return high, low, turns


def product(left, high, low):
    left_high = left.astype(jnp.bfloat16)
    left_low = (left - left_high.astype(jnp.float32)).astype(jnp.bfloat16)

    def dot(a, b):
        return jnp.dot(a, b, preferred_element_type=jnp.float32)

    return dot(left_high, high) + (dot(left_low, high) + dot(left_high, low))


def gate_kernel(streams_hbm, filter_hbm, upstream_hbm, out_ref, streams_ref, filter_ref, upstream_ref, arrived):
    devices, stacked, fast = out_ref.shape
    group = stacked // 3
    loads = [
        pltpu.make_async_copy(source, target, arrived.at[i])
        for i, (source, target) in enumerate(
            [(streams_hbm, streams_ref), (upstream_hbm, upstream_ref), (filter_hbm, filter_ref)]
        )
    ]
    for load in loads:
        load.start()
    for load in loads:
        load.wait()
    query_part = streams_ref[0].astype(jnp.float32)
    key_part = streams_ref[1].astype(jnp.float32)
    value_part = streams_ref[2].astype(jnp.float32)
    upstream = upstream_ref[...].astype(jnp.float32)
    out_ref[:, :group] = (key_part * value_part).reshape(devices, group, fast)
    out_ref[:, group : 2 * group] = filter_ref[...].reshape(devices, group, fast)
    out_ref[:, 2 * group :] = (query_part * upstream).reshape(devices, group, fast)


def convolve_kernel(signal_ref, high_ref, low_ref, turns_ref, out_ref):
    devices, stacked, fast = signal_ref.shape
    slow, group = 2 * devices, stacked // 3
    count = devices + 1

    def turn(which, k):
        return turns_ref[which * count + k : which * count + k + 1, :]

    signal = [signal_ref[a] for a in range(devices)]
    real, imag = [None] * count, [None] * count
    for k in range(devices // 2 + 1):
        sums = [
            weighted([(circle(slow, a * k)[part], signal[a]) for a in range(parity, devices, 2)])
            for part in range(2)
            for parity in range(2)
        ]
        cos_even, cos_odd, sin_even, sin_odd = sums
        real[k] = weighted([(1.0, cos_even), (1.0, cos_odd)])
        imag[k] = weighted([(-1.0, sin_even), (-1.0, sin_odd)])
        if 2 * k != devices:
            real[devices - k] = weighted([(1.0, cos_even), (-1.0, cos_odd)])
            imag[devices - k] = weighted([(1.0, sin_even), (-1.0, sin_odd)])
    rows = []
    for k in range(count):
        cos, sin = turn(0, k), turn(1, k)
        if k == 0:
            turned = (real[k], jnp.zeros_like(real[k]))
        elif imag[k] is None:
            turned = (real[k] * cos, -(real[k] * sin))
        else:
            turned = (real[k] * cos + imag[k] * sin, imag[k] * cos - real[k] * sin)
        rows.append(jnp.concatenate(turned, axis=1))
    high, low = high_ref[...], low_ref[...]
    spectrum = product(jnp.concatenate(rows, axis=0), high, low)
    rows = []
    for k in range(count):
        base = k * stacked
        parts = [spectrum[base + i * group : base + (i + 1) * group] for i in range(3)]
        (gated_real, taps_real, grad_real) = (p[:, :fast] for p in parts)
        (gated_imag, taps_imag, grad_imag) = (p[:, fast:] for p in parts)
        rows.append(
            jnp.concatenate(
                [
                    jnp.concatenate(
                        [
                            gated_real * taps_real - gated_imag * taps_imag,
                            -(gated_real * taps_imag + gated_imag * taps_real),
                        ],
                        axis=1,
                    ),
                    jnp.concatenate(
                        [
                            grad_real * taps_real + grad_imag * taps_imag,
                            grad_real * taps_imag - grad_imag * taps_real,
                        ],
                        axis=1,
                    ),
                    jnp.concatenate(
                        [
                            grad_real * gated_real + grad_imag * gated_imag,
                            grad_real * gated_imag - grad_imag * gated_real,
                        ],
                        axis=1,
                    ),
                ],
                axis=0,
            )
        )
    back = product(jnp.concatenate(rows, axis=0), high, low)
    real, imag = [], []
    for k in range(count):
        cos, sin = turn(2, k), turn(3, k)
        row = back[k * stacked : (k + 1) * stacked]
        real.append(row[:, :fast] * cos + row[:, fast:] * sin)
        imag.append(row[:, fast:] * cos - row[:, :fast] * sin)
    half = devices // 2
    for parity in range(2):
        sign = 1.0 - 2.0 * parity
        cos_part = [weighted([(1.0, real[k]), (sign, real[devices - k])]) for k in range(half)]
        sin_part = [weighted([(1.0, imag[k]), (-sign, imag[devices - k])]) for k in range(half)]
        for a in range(parity, devices, 2):
            terms = [(circle(slow, a * k)[0], cos_part[k]) for k in range(half)]
            terms += [(circle(slow, a * k)[1], sin_part[k]) for k in range(1, half)]
            terms += [(circle(slow, a * half)[0], real[half]), (circle(slow, a * half)[1], imag[half])]
            out_ref[a] = weighted(terms)


def output_kernel(back_ref, streams_ref, upstream_ref, mixed_ref, streams_grad_ref, filter_grad_ref):
    channels, fast = filter_grad_ref.shape
    group = back_ref.shape[1] // 3
    long_conv = back_ref[:, :group].reshape(channels, fast)
    grad_gated = back_ref[:, group : 2 * group].reshape(channels, fast)
    filter_grad_ref[...] = back_ref[:, 2 * group :].reshape(channels, fast)
    mixed_ref[...] = (streams_ref[0].astype(jnp.float32) * long_conv).astype(jnp.bfloat16)
    streams_grad_ref[0] = (upstream_ref[...].astype(jnp.float32) * long_conv).astype(jnp.bfloat16)
    streams_grad_ref[1] = (streams_ref[2].astype(jnp.float32) * grad_gated).astype(jnp.bfloat16)
    streams_grad_ref[2] = (streams_ref[1].astype(jnp.float32) * grad_gated).astype(jnp.bfloat16)


def by_channel(streams, filter_raw, grad_output):
    devices = lax.axis_size("ctx")
    channels, fast = filter_raw.shape
    stacked = 3 * (channels // devices)
    tap_scale = 1.0 / math.sqrt(fast * devices)
    vmem = pl.BlockSpec(memory_space=pltpu.VMEM)
    params = pltpu.CompilerParams(vmem_limit_bytes=8 << 20)
    regrouped = jax.ShapeDtypeStruct((devices, stacked, fast), jnp.float32)
    signals = pl.pallas_call(
        gate_kernel,
        out_shape=regrouped,
        in_specs=[pl.BlockSpec(memory_space=pltpu.HBM)] * 3,
        out_specs=vmem,
        scratch_shapes=[
            pltpu.VMEM(streams.shape, streams.dtype),
            pltpu.VMEM(filter_raw.shape, filter_raw.dtype),
            pltpu.VMEM(grad_output.shape, grad_output.dtype),
            pltpu.SemaphoreType.DMA((3,)),
        ],
        compiler_params=params,
    )(*(pltpu.with_memory_space_constraint(x, pltpu.HBM) for x in (streams, filter_raw, grad_output)))
    signals = lax.all_to_all(signals, "ctx", split_axis=0, concat_axis=0, tiled=True)
    tables = transform_tables(devices, fast, tap_scale)
    results = pl.pallas_call(convolve_kernel, out_shape=regrouped, in_specs=[vmem] * 4, out_specs=vmem, compiler_params=params)(
        signals, *tables
    )
    results = lax.all_to_all(results, "ctx", split_axis=0, concat_axis=0, tiled=True)
    return pl.pallas_call(
        output_kernel,
        out_shape=(
            jax.ShapeDtypeStruct((channels, fast), jnp.bfloat16),
            jax.ShapeDtypeStruct((3, channels, fast), jnp.bfloat16),
            jax.ShapeDtypeStruct((channels, fast), jnp.float32),
        ),
        in_specs=[vmem] * 3,
        out_specs=(vmem,) * 3,
        compiler_params=params,
    )(results, streams, grad_output)


def local(streams, filter_raw, grad_output):
    devices = lax.axis_size("ctx")
    channels, fast = filter_raw.shape
    if devices % 2 == 0 and channels % (8 * devices) == 0 and fast % 128 == 0:
        return by_channel(streams, filter_raw, grad_output)
    return by_residue(streams, filter_raw, grad_output)


def solution(mesh):
    in_specs = (P(None, "tp", "ctx"), P("tp", "ctx"), P("tp", "ctx"))
    out_specs = (P("tp", "ctx"), P(None, "tp", "ctx"), P("tp", "ctx"))
    return jax.shard_map(local, mesh=mesh, in_specs=in_specs, out_specs=out_specs, check_vma=False)
```

```python
import math

import jax
import jax.numpy as jnp
import numpy as np
from jax import lax
from jax.experimental import pallas as pl
from jax.experimental.pallas import tpu as pltpu
from jax.sharding import PartitionSpec as P

highest = lax.Precision.HIGHEST


def dft_tables(slow, fast, devices, position):
    length = slow * fast
    stride = fast // devices
    freq_slow = jnp.arange(slow, dtype=jnp.int32)
    rows_slow = jnp.arange(devices, dtype=jnp.int32)
    angle_slow = (
        2.0 * math.pi / slow * (freq_slow[:, None] * rows_slow[None, :] % slow).astype(jnp.float32)
    )
    cols_twist = position * stride + jnp.arange(stride, dtype=jnp.int32)
    angle_twist = (
        2.0
        * math.pi
        / length
        * (freq_slow[:, None] * cols_twist[None, :] % length).astype(jnp.float32)
    )
    freq_fast = jnp.arange(fast, dtype=jnp.int32)
    angle_fast = (
        2.0 * math.pi / fast * (freq_fast[:, None] * freq_fast[None, :] % fast).astype(jnp.float32)
    )
    return (
        jnp.cos(angle_slow),
        jnp.sin(angle_slow),
        jnp.cos(angle_twist)[:, None, :],
        jnp.sin(angle_twist)[:, None, :],
        jnp.cos(angle_fast),
        jnp.sin(angle_fast),
    )


def forward_spectrum(signal, tables):
    cos_slow, sin_slow, cos_twist, sin_twist, cos_fast, sin_fast = tables
    stacked, channels, fast = signal.shape
    slow, devices = cos_slow.shape
    stride = fast // devices
    columns = lax.all_to_all(signal[:, None], "ctx", split_axis=3, concat_axis=1, tiled=True)
    flat = columns.reshape(stacked, devices, channels * stride)
    real_part = jnp.einsum("ka,sam->skm", cos_slow, flat, precision=highest).reshape(
        stacked, slow, channels, stride
    )
    imag_part = -jnp.einsum("ka,sam->skm", sin_slow, flat, precision=highest).reshape(
        stacked, slow, channels, stride
    )
    turned_real = real_part * cos_twist + imag_part * sin_twist
    turned_imag = imag_part * cos_twist - real_part * sin_twist
    rows_real, rows_imag = (
        lax.all_to_all(turned_real, "ctx", split_axis=1, concat_axis=3, tiled=True),
        lax.all_to_all(turned_imag, "ctx", split_axis=1, concat_axis=3, tiled=True),
    )
    spec_real = jnp.matmul(rows_real, cos_fast, precision=highest) + jnp.matmul(
        rows_imag, sin_fast, precision=highest
    )
    spec_imag = jnp.matmul(rows_imag, cos_fast, precision=highest) - jnp.matmul(
        rows_real, sin_fast, precision=highest
    )
    return (spec_real, spec_imag)


def inverse_signal(spec_real, spec_imag, tables):
    cos_slow, sin_slow, cos_twist, sin_twist, cos_fast, sin_fast = tables
    stacked, local_rows, channels, fast = spec_real.shape
    slow, devices = cos_slow.shape
    stride = fast // devices
    back_real = jnp.matmul(spec_real, cos_fast, precision=highest) - jnp.matmul(
        spec_imag, sin_fast, precision=highest
    )
    back_imag = jnp.matmul(spec_imag, cos_fast, precision=highest) + jnp.matmul(
        spec_real, sin_fast, precision=highest
    )
    cols_real, cols_imag = (
        lax.all_to_all(back_real, "ctx", split_axis=3, concat_axis=1, tiled=True),
        lax.all_to_all(back_imag, "ctx", split_axis=3, concat_axis=1, tiled=True),
    )
    turned_real = (cols_real * cos_twist - cols_imag * sin_twist).reshape(
        stacked, slow, channels * stride
    )
    turned_imag = (cols_imag * cos_twist + cols_real * sin_twist).reshape(
        stacked, slow, channels * stride
    )
    timeline = jnp.einsum("ka,skm->sam", cos_slow, turned_real, precision=highest) - jnp.einsum(
        "ka,skm->sam", sin_slow, turned_imag, precision=highest
    )
    timeline = timeline.reshape(stacked, devices, channels, stride)
    returned = lax.all_to_all(timeline, "ctx", split_axis=1, concat_axis=3, tiled=True)
    return returned[:, 0] / float(slow * fast)


def conv_product(gated_real, gated_imag, taps_real, taps_imag):
    conv_real = gated_real * taps_real - gated_imag * taps_imag
    conv_imag = gated_real * taps_imag + gated_imag * taps_real
    return (conv_real, conv_imag)


def corr_products(grad_real, grad_imag, gated_real, gated_imag, taps_real, taps_imag):
    corr_real = jnp.stack(
        [
            grad_real * taps_real + grad_imag * taps_imag,
            grad_real * gated_real + grad_imag * gated_imag,
        ]
    )
    corr_imag = jnp.stack(
        [
            grad_imag * taps_real - grad_real * taps_imag,
            grad_imag * gated_real - grad_real * gated_imag,
        ]
    )
    return (corr_real, corr_imag)


def by_residue(streams, filter_raw, grad_output):
    devices = lax.axis_size("ctx")
    position = lax.axis_index("ctx")
    channels, fast = filter_raw.shape
    slow = 2 * devices
    tap_scale = 1.0 / math.sqrt(fast * devices)
    tables = dft_tables(slow, fast, devices, position)
    query_part = streams[0].astype(jnp.float32)
    key_part = streams[1].astype(jnp.float32)
    value_part = streams[2].astype(jnp.float32)
    gated_input = key_part * value_part
    kernel_taps = filter_raw * tap_scale
    upstream = grad_output.astype(jnp.float32)
    grad_conv = query_part * upstream
    spec_real, spec_imag = forward_spectrum(jnp.stack([gated_input, kernel_taps]), tables)
    conv_real, conv_imag = conv_product(spec_real[0], spec_imag[0], spec_real[1], spec_imag[1])
    long_conv = inverse_signal(conv_real[None], conv_imag[None], tables)[0]
    grad_real, grad_imag = forward_spectrum(grad_conv[None], tables)
    corr_real, corr_imag = corr_products(
        grad_real[0], grad_imag[0], spec_real[0], spec_imag[0], spec_real[1], spec_imag[1]
    )
    both_back = inverse_signal(corr_real, corr_imag, tables)
    grad_gated = both_back[0]
    filter_back = both_back[1]
    grad_filter = filter_back * tap_scale
    mixed_out = (query_part * long_conv).astype(jnp.bfloat16)
    grad_query = (upstream * long_conv).astype(jnp.bfloat16)
    grad_key = (grad_gated * value_part).astype(jnp.bfloat16)
    grad_value = (grad_gated * key_part).astype(jnp.bfloat16)
    grad_streams = jnp.stack([grad_query, grad_key, grad_value], axis=0)
    return (mixed_out, grad_streams, grad_filter)


def table(angle):
    return np.cos(angle), np.sin(angle)


def circle(count, at):
    exact = {0: (1.0, 0.0), 1: (0.0, 1.0), 2: (-1.0, 0.0), 3: (0.0, -1.0)}
    at = at % count
    if 4 * at % count == 0:
        return exact[4 * at // count]
    return math.cos(2.0 * math.pi * at / count), math.sin(2.0 * math.pi * at / count)


def weighted(terms):
    total = None
    for weight, array in terms:
        if weight == 0.0 or array is None:
            continue
        if total is None:
            total = array if weight == 1.0 else -array if weight == -1.0 else array * weight
        elif weight == 1.0:
            total = total + array
        elif weight == -1.0:
            total = total - array
        else:
            total = total + array * weight
    return total


def transform_tables(devices, block, fast, scale):
    slow = 2 * devices
    length = slow * fast
    at = np.arange(fast)
    cos, sin = table(2.0 * np.pi / fast * (at[:, None] * at[None, :] % fast))
    matrix = np.block([[cos, -sin], [sin, cos]]).astype(np.float32)
    high = matrix.astype(jnp.bfloat16)
    low = (matrix - high.astype(np.float32)).astype(jnp.bfloat16)
    rows = np.arange(devices + 1)
    weight = np.where((rows == 0) | (rows == devices), 1.0, 2.0)[:, None] * scale / length
    turns = [np.concatenate(table(2.0 * np.pi / length * (rows[:, None] * at[None, :] % length)))]
    for first in range(0, devices, block):
        cos, sin = table(2.0 * np.pi / length * (rows[:, None] * (first * fast + at[None, :]) % length))
        turns.append(np.concatenate([cos * weight, sin * weight]))
    return high, low, np.stack(turns).astype(np.float32)


def by_partner(parts, place):
    parts = list(parts)
    step = 1
    while step < len(parts):
        crossed = (place & step) != 0
        parts = [jnp.where(crossed, parts[x ^ step], parts[x]) for x in range(len(parts))]
        step *= 2
    return parts


def product(left, high, low):
    left_high = left.astype(jnp.bfloat16)
    left_low = (left - left_high.astype(jnp.float32)).astype(jnp.bfloat16)

    def dot(a, b):
        return jnp.dot(a, b, preferred_element_type=jnp.float32)

    return dot(left_high, high) + (dot(left_low, high) + dot(left_high, low))


def gate_kernel(streams_hbm, filter_hbm, upstream_hbm, out_ref, streams_ref, filter_ref, upstream_ref, arrived):
    devices, stacked, fast = out_ref.shape
    group = stacked // 3
    loads = [
        pltpu.make_async_copy(source, target, arrived.at[i])
        for i, (source, target) in enumerate(
            [(streams_hbm, streams_ref), (upstream_hbm, upstream_ref), (filter_hbm, filter_ref)]
        )
    ]
    for load in loads:
        load.start()
    for load in loads:
        load.wait()
    query_part = streams_ref[0].astype(jnp.float32)
    key_part = streams_ref[1].astype(jnp.float32)
    value_part = streams_ref[2].astype(jnp.float32)
    upstream = upstream_ref[...].astype(jnp.float32)
    block = streams_ref.shape[1] // group
    for first in range(0, devices, block):
        out_ref[first : first + block, :group] = (key_part * value_part).reshape(block, group, fast)
        out_ref[first : first + block, group : 2 * group] = filter_ref[...].reshape(block, group, fast)
        out_ref[first : first + block, 2 * group :] = (query_part * upstream).reshape(block, group, fast)


def convolve_kernel(signal_ref, high_ref, low_ref, turns_ref, *out_refs):
    devices, stacked, fast = signal_ref.shape
    slow, group, block = 2 * devices, stacked // 3, len(out_refs)
    count = devices + 1
    position = lax.axis_index("ctx")

    def turn(which, k):
        return turns_ref[which, k : k + 1, :], turns_ref[which, count + k : count + k + 1, :]

    signal = [signal_ref[a] for a in range(devices)]
    real, imag = [None] * count, [None] * count
    for k in range(devices // 2 + 1):
        sums = [
            weighted([(circle(slow, a * k)[part], signal[a]) for a in range(parity, devices, 2)])
            for part in range(2)
            for parity in range(2)
        ]
        cos_even, cos_odd, sin_even, sin_odd = sums
        real[k] = weighted([(1.0, cos_even), (1.0, cos_odd)])
        imag[k] = weighted([(-1.0, sin_even), (-1.0, sin_odd)])
        if 2 * k != devices:
            real[devices - k] = weighted([(1.0, cos_even), (-1.0, cos_odd)])
            imag[devices - k] = weighted([(1.0, sin_even), (-1.0, sin_odd)])
    rows = []
    for k in range(count):
        cos, sin = turn(0, k)
        if k == 0:
            turned = (real[k], jnp.zeros_like(real[k]))
        elif imag[k] is None:
            turned = (real[k] * cos, -(real[k] * sin))
        else:
            turned = (real[k] * cos + imag[k] * sin, imag[k] * cos - real[k] * sin)
        rows.append(jnp.concatenate(turned, axis=1))
    high, low = high_ref[...], low_ref[...]
    spectrum = product(jnp.concatenate(rows, axis=0), high, low)
    rows = []
    for k in range(count):
        base = k * stacked
        parts = [spectrum[base + i * group : base + (i + 1) * group] for i in range(3)]
        (gated_real, taps_real, grad_real) = (p[:, :fast] for p in parts)
        (gated_imag, taps_imag, grad_imag) = (p[:, fast:] for p in parts)
        rows.append(
            jnp.concatenate(
                [
                    jnp.concatenate(
                        [
                            gated_real * taps_real - gated_imag * taps_imag,
                            -(gated_real * taps_imag + gated_imag * taps_real),
                        ],
                        axis=1,
                    ),
                    jnp.concatenate(
                        [
                            grad_real * taps_real + grad_imag * taps_imag,
                            grad_real * taps_imag - grad_imag * taps_real,
                        ],
                        axis=1,
                    ),
                    jnp.concatenate(
                        [
                            grad_real * gated_real + grad_imag * gated_imag,
                            grad_real * gated_imag - grad_imag * gated_real,
                        ],
                        axis=1,
                    ),
                ],
                axis=0,
            )
        )
    back = product(jnp.concatenate(rows, axis=0), high, low)
    real, imag = [], []
    for k in range(count):
        cos, sin = turn(1 + position // block, k)
        row = back[k * stacked : (k + 1) * stacked]
        real.append(row[:, :fast] * cos + row[:, fast:] * sin)
        imag.append(row[:, fast:] * cos - row[:, :fast] * sin)
    half = devices // 2
    results = [None] * block
    for parity in range(2):
        sign = 1.0 - 2.0 * parity
        cos_part = [weighted([(1.0, real[k]), (sign, real[devices - k])]) for k in range(half)]
        sin_part = [weighted([(1.0, imag[k]), (-sign, imag[devices - k])]) for k in range(half)]
        for a in range(parity, block, 2):
            terms = [(circle(slow, a * k)[0], cos_part[k]) for k in range(half)]
            terms += [(circle(slow, a * k)[1], sin_part[k]) for k in range(1, half)]
            terms += [(circle(slow, a * half)[0], real[half]), (circle(slow, a * half)[1], imag[half])]
            results[a] = weighted(terms)
    for out_ref, result in zip(out_refs, by_partner(results, position % block), strict=True):
        out_ref[...] = result


def output_kernel(streams_ref, upstream_ref, *refs):
    back_refs, (mixed_ref, streams_grad_ref, filter_grad_ref) = refs[:-3], refs[-3:]
    channels, _ = filter_grad_ref.shape
    block = len(back_refs)
    group = channels // block
    parts = by_partner([ref[...] for ref in back_refs], lax.axis_index("ctx") % block)
    long_conv = jnp.concatenate([part[:group] for part in parts], axis=0)
    grad_gated = jnp.concatenate([part[group : 2 * group] for part in parts], axis=0)
    filter_grad_ref[...] = jnp.concatenate([part[2 * group :] for part in parts], axis=0)
    mixed_ref[...] = (streams_ref[0].astype(jnp.float32) * long_conv).astype(jnp.bfloat16)
    streams_grad_ref[0] = (upstream_ref[...].astype(jnp.float32) * long_conv).astype(jnp.bfloat16)
    streams_grad_ref[1] = (streams_ref[2].astype(jnp.float32) * grad_gated).astype(jnp.bfloat16)
    streams_grad_ref[2] = (streams_ref[1].astype(jnp.float32) * grad_gated).astype(jnp.bfloat16)


def by_channel(streams, filter_raw, grad_output, block):
    devices = lax.axis_size("ctx")
    channels, fast = filter_raw.shape
    stacked = 3 * (channels // block)
    tap_scale = 1.0 / math.sqrt(fast * devices)
    vmem = pl.BlockSpec(memory_space=pltpu.VMEM)
    params = pltpu.CompilerParams(vmem_limit_bytes=8 << 20)
    signals = pl.pallas_call(
        gate_kernel,
        out_shape=jax.ShapeDtypeStruct((devices, stacked, fast), jnp.float32),
        in_specs=[pl.BlockSpec(memory_space=pltpu.HBM)] * 3,
        out_specs=vmem,
        scratch_shapes=[
            pltpu.VMEM(streams.shape, streams.dtype),
            pltpu.VMEM(filter_raw.shape, filter_raw.dtype),
            pltpu.VMEM(grad_output.shape, grad_output.dtype),
            pltpu.SemaphoreType.DMA((3,)),
        ],
        compiler_params=params,
    )(*(pltpu.with_memory_space_constraint(x, pltpu.HBM) for x in (streams, filter_raw, grad_output)))
    signals = lax.all_to_all(signals, "ctx", split_axis=0, concat_axis=0, tiled=True)
    results = pl.pallas_call(
        convolve_kernel,
        out_shape=[jax.ShapeDtypeStruct((stacked, fast), jnp.float32)] * block,
        in_specs=[vmem] * 4,
        out_specs=[vmem] * block,
        compiler_params=params,
    )(signals, *transform_tables(devices, block, fast, tap_scale))
    results = [
        result if x == 0 else lax.ppermute(result, "ctx", [(i, i ^ x) for i in range(devices)])
        for x, result in enumerate(results)
    ]
    return pl.pallas_call(
        output_kernel,
        out_shape=(
            jax.ShapeDtypeStruct((channels, fast), jnp.bfloat16),
            jax.ShapeDtypeStruct((3, channels, fast), jnp.bfloat16),
            jax.ShapeDtypeStruct((channels, fast), jnp.float32),
        ),
        in_specs=[vmem] * (2 + block),
        out_specs=(vmem,) * 3,
        compiler_params=params,
    )(streams, grad_output, *results)


def local(streams, filter_raw, grad_output):
    devices = lax.axis_size("ctx")
    channels, fast = filter_raw.shape
    block = 4
    if devices % block == 0 and devices <= 16 and channels % (16 * block) == 0 and fast % 128 == 0:
        return by_channel(streams, filter_raw, grad_output, block)
    return by_residue(streams, filter_raw, grad_output)


def solution(mesh):
    in_specs = (P(None, "tp", "ctx"), P("tp", "ctx"), P("tp", "ctx"))
    out_specs = (P("tp", "ctx"), P(None, "tp", "ctx"), P("tp", "ctx"))
    return jax.shard_map(local, mesh=mesh, in_specs=in_specs, out_specs=out_specs, check_vma=False)
```

```python
import math

import jax
import jax.numpy as jnp
import numpy as np
from jax import lax
from jax.experimental import pallas as pl
from jax.experimental.pallas import tpu as pltpu
from jax.sharding import PartitionSpec as P

highest = lax.Precision.HIGHEST


def dft_tables(slow, fast, devices, position):
    length = slow * fast
    stride = fast // devices
    freq_slow = jnp.arange(slow, dtype=jnp.int32)
    rows_slow = jnp.arange(devices, dtype=jnp.int32)
    angle_slow = (
        2.0 * math.pi / slow * (freq_slow[:, None] * rows_slow[None, :] % slow).astype(jnp.float32)
    )
    cols_twist = position * stride + jnp.arange(stride, dtype=jnp.int32)
    angle_twist = (
        2.0
        * math.pi
        / length
        * (freq_slow[:, None] * cols_twist[None, :] % length).astype(jnp.float32)
    )
    freq_fast = jnp.arange(fast, dtype=jnp.int32)
    angle_fast = (
        2.0 * math.pi / fast * (freq_fast[:, None] * freq_fast[None, :] % fast).astype(jnp.float32)
    )
    return (
        jnp.cos(angle_slow),
        jnp.sin(angle_slow),
        jnp.cos(angle_twist)[:, None, :],
        jnp.sin(angle_twist)[:, None, :],
        jnp.cos(angle_fast),
        jnp.sin(angle_fast),
    )


def forward_spectrum(signal, tables):
    cos_slow, sin_slow, cos_twist, sin_twist, cos_fast, sin_fast = tables
    stacked, channels, fast = signal.shape
    slow, devices = cos_slow.shape
    stride = fast // devices
    columns = lax.all_to_all(signal[:, None], "ctx", split_axis=3, concat_axis=1, tiled=True)
    flat = columns.reshape(stacked, devices, channels * stride)
    real_part = jnp.einsum("ka,sam->skm", cos_slow, flat, precision=highest).reshape(
        stacked, slow, channels, stride
    )
    imag_part = -jnp.einsum("ka,sam->skm", sin_slow, flat, precision=highest).reshape(
        stacked, slow, channels, stride
    )
    turned_real = real_part * cos_twist + imag_part * sin_twist
    turned_imag = imag_part * cos_twist - real_part * sin_twist
    rows_real, rows_imag = (
        lax.all_to_all(turned_real, "ctx", split_axis=1, concat_axis=3, tiled=True),
        lax.all_to_all(turned_imag, "ctx", split_axis=1, concat_axis=3, tiled=True),
    )
    spec_real = jnp.matmul(rows_real, cos_fast, precision=highest) + jnp.matmul(
        rows_imag, sin_fast, precision=highest
    )
    spec_imag = jnp.matmul(rows_imag, cos_fast, precision=highest) - jnp.matmul(
        rows_real, sin_fast, precision=highest
    )
    return (spec_real, spec_imag)


def inverse_signal(spec_real, spec_imag, tables):
    cos_slow, sin_slow, cos_twist, sin_twist, cos_fast, sin_fast = tables
    stacked, local_rows, channels, fast = spec_real.shape
    slow, devices = cos_slow.shape
    stride = fast // devices
    back_real = jnp.matmul(spec_real, cos_fast, precision=highest) - jnp.matmul(
        spec_imag, sin_fast, precision=highest
    )
    back_imag = jnp.matmul(spec_imag, cos_fast, precision=highest) + jnp.matmul(
        spec_real, sin_fast, precision=highest
    )
    cols_real, cols_imag = (
        lax.all_to_all(back_real, "ctx", split_axis=3, concat_axis=1, tiled=True),
        lax.all_to_all(back_imag, "ctx", split_axis=3, concat_axis=1, tiled=True),
    )
    turned_real = (cols_real * cos_twist - cols_imag * sin_twist).reshape(
        stacked, slow, channels * stride
    )
    turned_imag = (cols_imag * cos_twist + cols_real * sin_twist).reshape(
        stacked, slow, channels * stride
    )
    timeline = jnp.einsum("ka,skm->sam", cos_slow, turned_real, precision=highest) - jnp.einsum(
        "ka,skm->sam", sin_slow, turned_imag, precision=highest
    )
    timeline = timeline.reshape(stacked, devices, channels, stride)
    returned = lax.all_to_all(timeline, "ctx", split_axis=1, concat_axis=3, tiled=True)
    return returned[:, 0] / float(slow * fast)


def conv_product(gated_real, gated_imag, taps_real, taps_imag):
    conv_real = gated_real * taps_real - gated_imag * taps_imag
    conv_imag = gated_real * taps_imag + gated_imag * taps_real
    return (conv_real, conv_imag)


def corr_products(grad_real, grad_imag, gated_real, gated_imag, taps_real, taps_imag):
    corr_real = jnp.stack(
        [
            grad_real * taps_real + grad_imag * taps_imag,
            grad_real * gated_real + grad_imag * gated_imag,
        ]
    )
    corr_imag = jnp.stack(
        [
            grad_imag * taps_real - grad_real * taps_imag,
            grad_imag * gated_real - grad_real * gated_imag,
        ]
    )
    return (corr_real, corr_imag)


def by_residue(streams, filter_raw, grad_output):
    devices = lax.axis_size("ctx")
    position = lax.axis_index("ctx")
    channels, fast = filter_raw.shape
    slow = 2 * devices
    tap_scale = 1.0 / math.sqrt(fast * devices)
    tables = dft_tables(slow, fast, devices, position)
    query_part = streams[0].astype(jnp.float32)
    key_part = streams[1].astype(jnp.float32)
    value_part = streams[2].astype(jnp.float32)
    gated_input = key_part * value_part
    kernel_taps = filter_raw * tap_scale
    upstream = grad_output.astype(jnp.float32)
    grad_conv = query_part * upstream
    spec_real, spec_imag = forward_spectrum(jnp.stack([gated_input, kernel_taps]), tables)
    conv_real, conv_imag = conv_product(spec_real[0], spec_imag[0], spec_real[1], spec_imag[1])
    long_conv = inverse_signal(conv_real[None], conv_imag[None], tables)[0]
    grad_real, grad_imag = forward_spectrum(grad_conv[None], tables)
    corr_real, corr_imag = corr_products(
        grad_real[0], grad_imag[0], spec_real[0], spec_imag[0], spec_real[1], spec_imag[1]
    )
    both_back = inverse_signal(corr_real, corr_imag, tables)
    grad_gated = both_back[0]
    filter_back = both_back[1]
    grad_filter = filter_back * tap_scale
    mixed_out = (query_part * long_conv).astype(jnp.bfloat16)
    grad_query = (upstream * long_conv).astype(jnp.bfloat16)
    grad_key = (grad_gated * value_part).astype(jnp.bfloat16)
    grad_value = (grad_gated * key_part).astype(jnp.bfloat16)
    grad_streams = jnp.stack([grad_query, grad_key, grad_value], axis=0)
    return (mixed_out, grad_streams, grad_filter)


def table(angle):
    return np.cos(angle), np.sin(angle)


def circle(count, at):
    exact = {0: (1.0, 0.0), 1: (0.0, 1.0), 2: (-1.0, 0.0), 3: (0.0, -1.0)}
    at = at % count
    if 4 * at % count == 0:
        return exact[4 * at // count]
    return math.cos(2.0 * math.pi * at / count), math.sin(2.0 * math.pi * at / count)


def weighted(terms):
    total = None
    for weight, array in terms:
        if weight == 0.0 or array is None:
            continue
        if total is None:
            total = array if weight == 1.0 else -array if weight == -1.0 else array * weight
        elif weight == 1.0:
            total = total + array
        elif weight == -1.0:
            total = total - array
        else:
            total = total + array * weight
    return total


def transform_tables(devices, block, fast, scale):
    slow = 2 * devices
    length = slow * fast
    at = np.arange(fast)
    cos, sin = table(2.0 * np.pi / fast * (at[:, None] * at[None, :] % fast))
    matrix = np.block([[cos, -sin], [sin, cos]]).astype(np.float32)
    high = matrix.astype(jnp.bfloat16)
    low = (matrix - high.astype(np.float32)).astype(jnp.bfloat16)
    rows = np.arange(devices + 1)
    weight = np.where((rows == 0) | (rows == devices), 1.0, 2.0)[:, None] * scale / length
    turns = [np.concatenate(table(2.0 * np.pi / length * (rows[:, None] * at[None, :] % length)))]
    for first in range(0, devices, block):
        cos, sin = table(2.0 * np.pi / length * (rows[:, None] * (first * fast + at[None, :]) % length))
        turns.append(np.concatenate([cos * weight, sin * weight]))
    return high, low, np.stack(turns).astype(np.float32)


def by_partner(parts, place):
    parts = list(parts)
    step = 1
    while step < len(parts):
        crossed = (place & step) != 0
        parts = [jnp.where(crossed, parts[x ^ step], parts[x]) for x in range(len(parts))]
        step *= 2
    return parts


def product(left, high, low):
    left_high = left.astype(jnp.bfloat16)
    left_low = (left - left_high.astype(jnp.float32)).astype(jnp.bfloat16)

    def dot(a, b):
        return jnp.dot(a, b, preferred_element_type=jnp.float32)

    half = left.shape[0] // 2 // 16 * 16
    return jnp.concatenate(
        [
            dot(left_high[part], high) + (dot(left_low[part], high) + dot(left_high[part], low))
            for part in (slice(0, half), slice(half, left.shape[0]))
        ],
        axis=0,
    )


def gate_kernel(streams_hbm, filter_hbm, upstream_hbm, out_ref, streams_ref, filter_ref, upstream_ref, arrived):
    devices, stacked, fast = out_ref.shape
    group = stacked // 3
    loads = [
        pltpu.make_async_copy(source, target, arrived.at[i])
        for i, (source, target) in enumerate(
            [(streams_hbm, streams_ref), (upstream_hbm, upstream_ref), (filter_hbm, filter_ref)]
        )
    ]
    for load in loads:
        load.start()
    for load in loads:
        load.wait()
    query_part = streams_ref[0].astype(jnp.float32)
    key_part = streams_ref[1].astype(jnp.float32)
    value_part = streams_ref[2].astype(jnp.float32)
    upstream = upstream_ref[...].astype(jnp.float32)
    block = streams_ref.shape[1] // group
    for first in range(0, devices, block):
        out_ref[first : first + block, :group] = (key_part * value_part).reshape(block, group, fast)
        out_ref[first : first + block, group : 2 * group] = filter_ref[...].reshape(block, group, fast)
        out_ref[first : first + block, 2 * group :] = (query_part * upstream).reshape(block, group, fast)


def convolve_kernel(signal_ref, high_ref, low_ref, turns_ref, *out_refs):
    devices, stacked, fast = signal_ref.shape
    slow, group, block = 2 * devices, stacked // 3, len(out_refs)
    count = devices + 1
    position = lax.axis_index("ctx")

    def turn(which, k):
        return turns_ref[which, k : k + 1, :], turns_ref[which, count + k : count + k + 1, :]

    signal = [signal_ref[a] for a in range(devices)]
    real, imag = [None] * count, [None] * count
    for k in range(devices // 2 + 1):
        sums = [
            weighted([(circle(slow, a * k)[part], signal[a]) for a in range(parity, devices, 2)])
            for part in range(2)
            for parity in range(2)
        ]
        cos_even, cos_odd, sin_even, sin_odd = sums
        real[k] = weighted([(1.0, cos_even), (1.0, cos_odd)])
        imag[k] = weighted([(-1.0, sin_even), (-1.0, sin_odd)])
        if 2 * k != devices:
            real[devices - k] = weighted([(1.0, cos_even), (-1.0, cos_odd)])
            imag[devices - k] = weighted([(1.0, sin_even), (-1.0, sin_odd)])
    rows = []
    for k in range(count):
        cos, sin = turn(0, k)
        if k == 0:
            turned = (real[k], jnp.zeros_like(real[k]))
        elif imag[k] is None:
            turned = (real[k] * cos, -(real[k] * sin))
        else:
            turned = (real[k] * cos + imag[k] * sin, imag[k] * cos - real[k] * sin)
        rows.append(jnp.concatenate(turned, axis=1))
    high, low = high_ref[...], low_ref[...]
    spectrum = product(jnp.concatenate(rows, axis=0), high, low)
    rows = []
    for k in range(count):
        base = k * stacked
        parts = [spectrum[base + i * group : base + (i + 1) * group] for i in range(3)]
        (gated_real, taps_real, grad_real) = (p[:, :fast] for p in parts)
        (gated_imag, taps_imag, grad_imag) = (p[:, fast:] for p in parts)
        rows.append(
            jnp.concatenate(
                [
                    jnp.concatenate(
                        [
                            gated_real * taps_real - gated_imag * taps_imag,
                            -(gated_real * taps_imag + gated_imag * taps_real),
                        ],
                        axis=1,
                    ),
                    jnp.concatenate(
                        [
                            grad_real * taps_real + grad_imag * taps_imag,
                            grad_real * taps_imag - grad_imag * taps_real,
                        ],
                        axis=1,
                    ),
                    jnp.concatenate(
                        [
                            grad_real * gated_real + grad_imag * gated_imag,
                            grad_real * gated_imag - grad_imag * gated_real,
                        ],
                        axis=1,
                    ),
                ],
                axis=0,
            )
        )
    back = product(jnp.concatenate(rows, axis=0), high, low)
    real, imag = [], []
    for k in range(count):
        cos, sin = turn(1 + position // block, k)
        row = back[k * stacked : (k + 1) * stacked]
        real.append(row[:, :fast] * cos + row[:, fast:] * sin)
        imag.append(row[:, fast:] * cos - row[:, :fast] * sin)
    half = devices // 2
    results = [None] * block
    for parity in range(2):
        sign = 1.0 - 2.0 * parity
        cos_part = [weighted([(1.0, real[k]), (sign, real[devices - k])]) for k in range(half)]
        sin_part = [weighted([(1.0, imag[k]), (-sign, imag[devices - k])]) for k in range(half)]
        for a in range(parity, block, 2):
            terms = [(circle(slow, a * k)[0], cos_part[k]) for k in range(half)]
            terms += [(circle(slow, a * k)[1], sin_part[k]) for k in range(1, half)]
            terms += [(circle(slow, a * half)[0], real[half]), (circle(slow, a * half)[1], imag[half])]
            results[a] = weighted(terms)
    for out_ref, result in zip(out_refs, by_partner(results, position % block), strict=True):
        out_ref[...] = result


def output_kernel(streams_ref, upstream_ref, *refs):
    back_refs, (mixed_ref, streams_grad_ref, filter_grad_ref) = refs[:-3], refs[-3:]
    channels, _ = filter_grad_ref.shape
    block = len(back_refs)
    group = channels // block
    parts = by_partner([back_refs[k][...] for k in [0, 2, 3, 1]], lax.axis_index("ctx") % block)
    long_conv = jnp.concatenate([part[:group] for part in parts], axis=0)
    grad_gated = jnp.concatenate([part[group : 2 * group] for part in parts], axis=0)
    filter_grad_ref[...] = jnp.concatenate([part[2 * group :] for part in parts], axis=0)
    mixed_ref[...] = (streams_ref[0].astype(jnp.float32) * long_conv).astype(jnp.bfloat16)
    streams_grad_ref[0] = (upstream_ref[...].astype(jnp.float32) * long_conv).astype(jnp.bfloat16)
    streams_grad_ref[1] = (streams_ref[2].astype(jnp.float32) * grad_gated).astype(jnp.bfloat16)
    streams_grad_ref[2] = (streams_ref[1].astype(jnp.float32) * grad_gated).astype(jnp.bfloat16)


def by_channel(streams, filter_raw, grad_output, block):
    devices = lax.axis_size("ctx")
    channels, fast = filter_raw.shape
    stacked = 3 * (channels // block)
    tap_scale = 1.0 / math.sqrt(fast * devices)
    vmem = pl.BlockSpec(memory_space=pltpu.VMEM)
    params = pltpu.CompilerParams(vmem_limit_bytes=8 << 20)
    signals = pl.pallas_call(
        gate_kernel,
        out_shape=jax.ShapeDtypeStruct((devices, stacked, fast), jnp.float32),
        in_specs=[pl.BlockSpec(memory_space=pltpu.HBM)] * 3,
        out_specs=vmem,
        scratch_shapes=[
            pltpu.VMEM(streams.shape, streams.dtype),
            pltpu.VMEM(filter_raw.shape, filter_raw.dtype),
            pltpu.VMEM(grad_output.shape, grad_output.dtype),
            pltpu.SemaphoreType.DMA((3,)),
        ],
        compiler_params=params,
    )(*(pltpu.with_memory_space_constraint(x, pltpu.HBM) for x in (streams, filter_raw, grad_output)))
    signals = lax.all_to_all(signals, "ctx", split_axis=0, concat_axis=0, tiled=True)
    results = pl.pallas_call(
        convolve_kernel,
        out_shape=[jax.ShapeDtypeStruct((stacked, fast), jnp.float32)] * block,
        in_specs=[vmem] * 4,
        out_specs=[vmem] * block,
        compiler_params=params,
    )(signals, *transform_tables(devices, block, fast, tap_scale))
    order = (3, 1, 2)
    results = list(results[:1]) + [lax.ppermute(results[x], "ctx", [(i, i ^ x) for i in range(devices)]) for x in order]
    return pl.pallas_call(
        output_kernel,
        out_shape=(
            jax.ShapeDtypeStruct((channels, fast), jnp.bfloat16),
            jax.ShapeDtypeStruct((3, channels, fast), jnp.bfloat16),
            jax.ShapeDtypeStruct((channels, fast), jnp.float32),
        ),
        in_specs=[vmem] * (2 + block),
        out_specs=(vmem,) * 3,
        compiler_params=params,
    )(streams, grad_output, *results)


def local(streams, filter_raw, grad_output):
    devices = lax.axis_size("ctx")
    channels, fast = filter_raw.shape
    block = 4
    if devices % block == 0 and devices <= 16 and channels % (16 * block) == 0 and fast % 128 == 0:
        return by_channel(streams, filter_raw, grad_output, block)
    return by_residue(streams, filter_raw, grad_output)


def solution(mesh):
    in_specs = (P(None, "tp", "ctx"), P("tp", "ctx"), P("tp", "ctx"))
    out_specs = (P("tp", "ctx"), P(None, "tp", "ctx"), P("tp", "ctx"))
    return jax.shard_map(local, mesh=mesh, in_specs=in_specs, out_specs=out_specs, check_vma=False)
```

```python
import math

import jax
import jax.numpy as jnp
import numpy as np
from jax import lax
from jax.experimental import pallas as pl
from jax.experimental.pallas import tpu as pltpu
from jax.sharding import PartitionSpec as P

highest = lax.Precision.HIGHEST


def dft_tables(slow, fast, devices, position):
    length = slow * fast
    stride = fast // devices
    freq_slow = jnp.arange(slow, dtype=jnp.int32)
    rows_slow = jnp.arange(devices, dtype=jnp.int32)
    angle_slow = (
        2.0 * math.pi / slow * (freq_slow[:, None] * rows_slow[None, :] % slow).astype(jnp.float32)
    )
    cols_twist = position * stride + jnp.arange(stride, dtype=jnp.int32)
    angle_twist = (
        2.0
        * math.pi
        / length
        * (freq_slow[:, None] * cols_twist[None, :] % length).astype(jnp.float32)
    )
    freq_fast = jnp.arange(fast, dtype=jnp.int32)
    angle_fast = (
        2.0 * math.pi / fast * (freq_fast[:, None] * freq_fast[None, :] % fast).astype(jnp.float32)
    )
    return (
        jnp.cos(angle_slow),
        jnp.sin(angle_slow),
        jnp.cos(angle_twist)[:, None, :],
        jnp.sin(angle_twist)[:, None, :],
        jnp.cos(angle_fast),
        jnp.sin(angle_fast),
    )


def forward_spectrum(signal, tables):
    cos_slow, sin_slow, cos_twist, sin_twist, cos_fast, sin_fast = tables
    stacked, channels, fast = signal.shape
    slow, devices = cos_slow.shape
    stride = fast // devices
    columns = lax.all_to_all(signal[:, None], "ctx", split_axis=3, concat_axis=1, tiled=True)
    flat = columns.reshape(stacked, devices, channels * stride)
    real_part = jnp.einsum("ka,sam->skm", cos_slow, flat, precision=highest).reshape(
        stacked, slow, channels, stride
    )
    imag_part = -jnp.einsum("ka,sam->skm", sin_slow, flat, precision=highest).reshape(
        stacked, slow, channels, stride
    )
    turned_real = real_part * cos_twist + imag_part * sin_twist
    turned_imag = imag_part * cos_twist - real_part * sin_twist
    rows_real, rows_imag = (
        lax.all_to_all(turned_real, "ctx", split_axis=1, concat_axis=3, tiled=True),
        lax.all_to_all(turned_imag, "ctx", split_axis=1, concat_axis=3, tiled=True),
    )
    spec_real = jnp.matmul(rows_real, cos_fast, precision=highest) + jnp.matmul(
        rows_imag, sin_fast, precision=highest
    )
    spec_imag = jnp.matmul(rows_imag, cos_fast, precision=highest) - jnp.matmul(
        rows_real, sin_fast, precision=highest
    )
    return (spec_real, spec_imag)


def inverse_signal(spec_real, spec_imag, tables):
    cos_slow, sin_slow, cos_twist, sin_twist, cos_fast, sin_fast = tables
    stacked, local_rows, channels, fast = spec_real.shape
    slow, devices = cos_slow.shape
    stride = fast // devices
    back_real = jnp.matmul(spec_real, cos_fast, precision=highest) - jnp.matmul(
        spec_imag, sin_fast, precision=highest
    )
    back_imag = jnp.matmul(spec_imag, cos_fast, precision=highest) + jnp.matmul(
        spec_real, sin_fast, precision=highest
    )
    cols_real, cols_imag = (
        lax.all_to_all(back_real, "ctx", split_axis=3, concat_axis=1, tiled=True),
        lax.all_to_all(back_imag, "ctx", split_axis=3, concat_axis=1, tiled=True),
    )
    turned_real = (cols_real * cos_twist - cols_imag * sin_twist).reshape(
        stacked, slow, channels * stride
    )
    turned_imag = (cols_imag * cos_twist + cols_real * sin_twist).reshape(
        stacked, slow, channels * stride
    )
    timeline = jnp.einsum("ka,skm->sam", cos_slow, turned_real, precision=highest) - jnp.einsum(
        "ka,skm->sam", sin_slow, turned_imag, precision=highest
    )
    timeline = timeline.reshape(stacked, devices, channels, stride)
    returned = lax.all_to_all(timeline, "ctx", split_axis=1, concat_axis=3, tiled=True)
    return returned[:, 0] / float(slow * fast)


def conv_product(gated_real, gated_imag, taps_real, taps_imag):
    conv_real = gated_real * taps_real - gated_imag * taps_imag
    conv_imag = gated_real * taps_imag + gated_imag * taps_real
    return (conv_real, conv_imag)


def corr_products(grad_real, grad_imag, gated_real, gated_imag, taps_real, taps_imag):
    corr_real = jnp.stack(
        [
            grad_real * taps_real + grad_imag * taps_imag,
            grad_real * gated_real + grad_imag * gated_imag,
        ]
    )
    corr_imag = jnp.stack(
        [
            grad_imag * taps_real - grad_real * taps_imag,
            grad_imag * gated_real - grad_real * gated_imag,
        ]
    )
    return (corr_real, corr_imag)


def by_residue(streams, filter_raw, grad_output):
    devices = lax.axis_size("ctx")
    position = lax.axis_index("ctx")
    channels, fast = filter_raw.shape
    slow = 2 * devices
    tap_scale = 1.0 / math.sqrt(fast * devices)
    tables = dft_tables(slow, fast, devices, position)
    query_part = streams[0].astype(jnp.float32)
    key_part = streams[1].astype(jnp.float32)
    value_part = streams[2].astype(jnp.float32)
    gated_input = key_part * value_part
    kernel_taps = filter_raw * tap_scale
    upstream = grad_output.astype(jnp.float32)
    grad_conv = query_part * upstream
    spec_real, spec_imag = forward_spectrum(jnp.stack([gated_input, kernel_taps]), tables)
    conv_real, conv_imag = conv_product(spec_real[0], spec_imag[0], spec_real[1], spec_imag[1])
    long_conv = inverse_signal(conv_real[None], conv_imag[None], tables)[0]
    grad_real, grad_imag = forward_spectrum(grad_conv[None], tables)
    corr_real, corr_imag = corr_products(
        grad_real[0], grad_imag[0], spec_real[0], spec_imag[0], spec_real[1], spec_imag[1]
    )
    both_back = inverse_signal(corr_real, corr_imag, tables)
    grad_gated = both_back[0]
    filter_back = both_back[1]
    grad_filter = filter_back * tap_scale
    mixed_out = (query_part * long_conv).astype(jnp.bfloat16)
    grad_query = (upstream * long_conv).astype(jnp.bfloat16)
    grad_key = (grad_gated * value_part).astype(jnp.bfloat16)
    grad_value = (grad_gated * key_part).astype(jnp.bfloat16)
    grad_streams = jnp.stack([grad_query, grad_key, grad_value], axis=0)
    return (mixed_out, grad_streams, grad_filter)


def table(angle):
    return np.cos(angle), np.sin(angle)


def circle(count, at):
    exact = {0: (1.0, 0.0), 1: (0.0, 1.0), 2: (-1.0, 0.0), 3: (0.0, -1.0)}
    at = at % count
    if 4 * at % count == 0:
        return exact[4 * at // count]
    return math.cos(2.0 * math.pi * at / count), math.sin(2.0 * math.pi * at / count)


def weighted(terms):
    total = None
    for weight, array in terms:
        if weight == 0.0 or array is None:
            continue
        if total is None:
            total = array if weight == 1.0 else -array if weight == -1.0 else array * weight
        elif weight == 1.0:
            total = total + array
        elif weight == -1.0:
            total = total - array
        else:
            total = total + array * weight
    return total


def transform_tables(devices, block, fast, scale):
    slow = 2 * devices
    length = slow * fast
    at = np.arange(fast)
    cos, sin = table(2.0 * np.pi / fast * (at[:, None] * at[None, :] % fast))
    matrix = np.block([[cos, -sin], [sin, cos]]).astype(np.float32)
    high = matrix.astype(jnp.bfloat16)
    low = (matrix - high.astype(np.float32)).astype(jnp.bfloat16)
    rows = np.arange(devices + 1)
    weight = np.where((rows == 0) | (rows == devices), 1.0, 2.0)[:, None] * scale / length
    turns = [np.concatenate(table(2.0 * np.pi / length * (rows[:, None] * at[None, :] % length)))]
    for first in range(0, devices, block):
        cos, sin = table(2.0 * np.pi / length * (rows[:, None] * (first * fast + at[None, :]) % length))
        turns.append(np.concatenate([cos * weight, sin * weight]))
    return high, low, np.stack(turns).astype(np.float32)


def by_partner(parts, place):
    parts = list(parts)
    step = 1
    while step < len(parts):
        crossed = (place & step) != 0
        parts = [jnp.where(crossed, parts[x ^ step], parts[x]) for x in range(len(parts))]
        step *= 2
    return parts


def product(left, high, low):
    left_high = left.astype(jnp.bfloat16)
    left_low = (left - left_high.astype(jnp.float32)).astype(jnp.bfloat16)

    def dot(a, b):
        return jnp.dot(a, b, preferred_element_type=jnp.float32)

    half = left.shape[0] // 2 // 16 * 16
    return jnp.concatenate(
        [
            dot(left_high[part], high) + (dot(left_low[part], high) + dot(left_high[part], low))
            for part in (slice(0, half), slice(half, left.shape[0]))
        ],
        axis=0,
    )


def exchange_order(devices):
    return [5, 1, 6, 0, 2, 4, 3, 7] if devices == 8 else list(range(devices))


def gate_kernel(streams_hbm, filter_hbm, upstream_hbm, out_ref, streams_ref, filter_ref, upstream_ref, arrived):
    devices, stacked, fast = out_ref.shape
    group = stacked // 3
    loads = [
        pltpu.make_async_copy(source, target, arrived.at[i])
        for i, (source, target) in enumerate(
            [(streams_hbm, streams_ref), (upstream_hbm, upstream_ref), (filter_hbm, filter_ref)]
        )
    ]
    for load in loads:
        load.start()
    for load in loads:
        load.wait()
    gated_input = streams_ref[1].astype(jnp.float32) * streams_ref[2].astype(jnp.float32)
    grad_conv = streams_ref[0].astype(jnp.float32) * upstream_ref[...].astype(jnp.float32)
    block = streams_ref.shape[1] // group
    for chunk, device in enumerate(exchange_order(devices)):
        share = slice(device % block * group, (device % block + 1) * group)
        out_ref[chunk, :group] = gated_input[share]
        out_ref[chunk, group : 2 * group] = filter_ref[share]
        out_ref[chunk, 2 * group :] = grad_conv[share]


def convolve_kernel(signal_ref, high_ref, low_ref, turns_ref, *out_refs):
    devices, stacked, fast = signal_ref.shape
    slow, group, block = 2 * devices, stacked // 3, len(out_refs)
    count = devices + 1
    position = lax.axis_index("ctx")

    def turn(which, k):
        return turns_ref[which, k : k + 1, :], turns_ref[which, count + k : count + k + 1, :]

    order = exchange_order(devices)
    signal = [signal_ref[order.index(a)] for a in range(devices)]
    real, imag = [None] * count, [None] * count
    for k in range(devices // 2 + 1):
        sums = [
            weighted([(circle(slow, a * k)[part], signal[a]) for a in range(parity, devices, 2)])
            for part in range(2)
            for parity in range(2)
        ]
        cos_even, cos_odd, sin_even, sin_odd = sums
        real[k] = weighted([(1.0, cos_even), (1.0, cos_odd)])
        imag[k] = weighted([(-1.0, sin_even), (-1.0, sin_odd)])
        if 2 * k != devices:
            real[devices - k] = weighted([(1.0, cos_even), (-1.0, cos_odd)])
            imag[devices - k] = weighted([(1.0, sin_even), (-1.0, sin_odd)])
    rows = []
    for k in range(count):
        cos, sin = turn(0, k)
        if k == 0:
            turned = (real[k], jnp.zeros_like(real[k]))
        elif imag[k] is None:
            turned = (real[k] * cos, -(real[k] * sin))
        else:
            turned = (real[k] * cos + imag[k] * sin, imag[k] * cos - real[k] * sin)
        rows.append(jnp.concatenate(turned, axis=1))
    high, low = high_ref[...], low_ref[...]
    spectrum = product(jnp.concatenate(rows, axis=0), high, low)
    rows = []
    for k in range(count):
        base = k * stacked
        parts = [spectrum[base + i * group : base + (i + 1) * group] for i in range(3)]
        (gated_real, taps_real, grad_real) = (p[:, :fast] for p in parts)
        (gated_imag, taps_imag, grad_imag) = (p[:, fast:] for p in parts)
        rows.append(
            jnp.concatenate(
                [
                    jnp.concatenate(
                        [
                            gated_real * taps_real - gated_imag * taps_imag,
                            -(gated_real * taps_imag + gated_imag * taps_real),
                        ],
                        axis=1,
                    ),
                    jnp.concatenate(
                        [
                            grad_real * taps_real + grad_imag * taps_imag,
                            grad_real * taps_imag - grad_imag * taps_real,
                        ],
                        axis=1,
                    ),
                    jnp.concatenate(
                        [
                            grad_real * gated_real + grad_imag * gated_imag,
                            grad_real * gated_imag - grad_imag * gated_real,
                        ],
                        axis=1,
                    ),
                ],
                axis=0,
            )
        )
    back = product(jnp.concatenate(rows, axis=0), high, low)
    real, imag = [], []
    for k in range(count):
        cos, sin = turn(1 + position // block, k)
        row = back[k * stacked : (k + 1) * stacked]
        real.append(row[:, :fast] * cos + row[:, fast:] * sin)
        imag.append(row[:, fast:] * cos - row[:, :fast] * sin)
    half = devices // 2
    results = [None] * block
    for parity in range(2):
        sign = 1.0 - 2.0 * parity
        cos_part = [weighted([(1.0, real[k]), (sign, real[devices - k])]) for k in range(half)]
        sin_part = [weighted([(1.0, imag[k]), (-sign, imag[devices - k])]) for k in range(half)]
        for a in range(parity, block, 2):
            terms = [(circle(slow, a * k)[0], cos_part[k]) for k in range(half)]
            terms += [(circle(slow, a * k)[1], sin_part[k]) for k in range(1, half)]
            terms += [(circle(slow, a * half)[0], real[half]), (circle(slow, a * half)[1], imag[half])]
            results[a] = weighted(terms)
    for out_ref, result in zip(out_refs, by_partner(results, position % block), strict=True):
        out_ref[...] = result


def output_kernel(streams_ref, upstream_ref, *refs):
    back_refs, (mixed_ref, streams_grad_ref, filter_grad_ref) = refs[:-3], refs[-3:]
    channels, _ = filter_grad_ref.shape
    block = len(back_refs)
    group = channels // block
    parts = by_partner([back_refs[k][...] for k in [0, 2, 3, 1]], lax.axis_index("ctx") % block)
    long_conv = jnp.concatenate([part[:group] for part in parts], axis=0)
    grad_gated = jnp.concatenate([part[group : 2 * group] for part in parts], axis=0)
    filter_grad_ref[...] = jnp.concatenate([part[2 * group :] for part in parts], axis=0)
    mixed_ref[...] = (streams_ref[0].astype(jnp.float32) * long_conv).astype(jnp.bfloat16)
    streams_grad_ref[0] = (upstream_ref[...].astype(jnp.float32) * long_conv).astype(jnp.bfloat16)
    streams_grad_ref[1] = (streams_ref[2].astype(jnp.float32) * grad_gated).astype(jnp.bfloat16)
    streams_grad_ref[2] = (streams_ref[1].astype(jnp.float32) * grad_gated).astype(jnp.bfloat16)


def by_channel(streams, filter_raw, grad_output, block):
    devices = lax.axis_size("ctx")
    channels, fast = filter_raw.shape
    stacked = 3 * (channels // block)
    tap_scale = 1.0 / math.sqrt(fast * devices)
    vmem = pl.BlockSpec(memory_space=pltpu.VMEM)
    params = pltpu.CompilerParams(vmem_limit_bytes=8 << 20)
    signals = pl.pallas_call(
        gate_kernel,
        out_shape=jax.ShapeDtypeStruct((devices, stacked, fast), jnp.float32),
        in_specs=[pl.BlockSpec(memory_space=pltpu.HBM)] * 3,
        out_specs=vmem,
        scratch_shapes=[
            pltpu.VMEM(streams.shape, streams.dtype),
            pltpu.VMEM(filter_raw.shape, filter_raw.dtype),
            pltpu.VMEM(grad_output.shape, grad_output.dtype),
            pltpu.SemaphoreType.DMA((3,)),
        ],
        compiler_params=params,
    )(*(pltpu.with_memory_space_constraint(x, pltpu.HBM) for x in (streams, filter_raw, grad_output)))
    signals = lax.all_to_all(
        signals, "ctx", split_axis=0, concat_axis=0, axis_index_groups=[exchange_order(devices)], tiled=True
    )
    results = pl.pallas_call(
        convolve_kernel,
        out_shape=[jax.ShapeDtypeStruct((stacked, fast), jnp.float32)] * block,
        in_specs=[vmem] * 4,
        out_specs=[vmem] * block,
        compiler_params=params,
    )(signals, *transform_tables(devices, block, fast, tap_scale))
    order = (3, 1, 2)
    results = list(results[:1]) + [lax.ppermute(results[x], "ctx", [(i, i ^ x) for i in range(devices)]) for x in order]
    return pl.pallas_call(
        output_kernel,
        out_shape=(
            jax.ShapeDtypeStruct((channels, fast), jnp.bfloat16),
            jax.ShapeDtypeStruct((3, channels, fast), jnp.bfloat16),
            jax.ShapeDtypeStruct((channels, fast), jnp.float32),
        ),
        in_specs=[vmem] * (2 + block),
        out_specs=(vmem,) * 3,
        compiler_params=params,
    )(streams, grad_output, *results)


def local(streams, filter_raw, grad_output):
    devices = lax.axis_size("ctx")
    channels, fast = filter_raw.shape
    block = 4
    if devices % block == 0 and devices <= 16 and channels % (16 * block) == 0 and fast % 128 == 0:
        return by_channel(streams, filter_raw, grad_output, block)
    return by_residue(streams, filter_raw, grad_output)


def solution(mesh):
    in_specs = (P(None, "tp", "ctx"), P("tp", "ctx"), P("tp", "ctx"))
    out_specs = (P("tp", "ctx"), P(None, "tp", "ctx"), P("tp", "ctx"))
    return jax.shard_map(local, mesh=mesh, in_specs=in_specs, out_specs=out_specs, check_vma=False)
```

```python
import math

import jax
import jax.numpy as jnp
import numpy as np
from jax import lax
from jax.experimental import pallas as pl
from jax.experimental.pallas import tpu as pltpu
from jax.sharding import PartitionSpec as P

highest = lax.Precision.HIGHEST


def dft_tables(slow, fast, devices, position):
    length = slow * fast
    stride = fast // devices
    freq_slow = jnp.arange(slow, dtype=jnp.int32)
    rows_slow = jnp.arange(devices, dtype=jnp.int32)
    angle_slow = (
        2.0 * math.pi / slow * (freq_slow[:, None] * rows_slow[None, :] % slow).astype(jnp.float32)
    )
    cols_twist = position * stride + jnp.arange(stride, dtype=jnp.int32)
    angle_twist = (
        2.0
        * math.pi
        / length
        * (freq_slow[:, None] * cols_twist[None, :] % length).astype(jnp.float32)
    )
    freq_fast = jnp.arange(fast, dtype=jnp.int32)
    angle_fast = (
        2.0 * math.pi / fast * (freq_fast[:, None] * freq_fast[None, :] % fast).astype(jnp.float32)
    )
    return (
        jnp.cos(angle_slow),
        jnp.sin(angle_slow),
        jnp.cos(angle_twist)[:, None, :],
        jnp.sin(angle_twist)[:, None, :],
        jnp.cos(angle_fast),
        jnp.sin(angle_fast),
    )


def forward_spectrum(signal, tables):
    cos_slow, sin_slow, cos_twist, sin_twist, cos_fast, sin_fast = tables
    stacked, channels, fast = signal.shape
    slow, devices = cos_slow.shape
    stride = fast // devices
    columns = lax.all_to_all(signal[:, None], "ctx", split_axis=3, concat_axis=1, tiled=True)
    flat = columns.reshape(stacked, devices, channels * stride)
    real_part = jnp.einsum("ka,sam->skm", cos_slow, flat, precision=highest).reshape(
        stacked, slow, channels, stride
    )
    imag_part = -jnp.einsum("ka,sam->skm", sin_slow, flat, precision=highest).reshape(
        stacked, slow, channels, stride
    )
    turned_real = real_part * cos_twist + imag_part * sin_twist
    turned_imag = imag_part * cos_twist - real_part * sin_twist
    rows_real, rows_imag = (
        lax.all_to_all(turned_real, "ctx", split_axis=1, concat_axis=3, tiled=True),
        lax.all_to_all(turned_imag, "ctx", split_axis=1, concat_axis=3, tiled=True),
    )
    spec_real = jnp.matmul(rows_real, cos_fast, precision=highest) + jnp.matmul(
        rows_imag, sin_fast, precision=highest
    )
    spec_imag = jnp.matmul(rows_imag, cos_fast, precision=highest) - jnp.matmul(
        rows_real, sin_fast, precision=highest
    )
    return (spec_real, spec_imag)


def inverse_signal(spec_real, spec_imag, tables):
    cos_slow, sin_slow, cos_twist, sin_twist, cos_fast, sin_fast = tables
    stacked, local_rows, channels, fast = spec_real.shape
    slow, devices = cos_slow.shape
    stride = fast // devices
    back_real = jnp.matmul(spec_real, cos_fast, precision=highest) - jnp.matmul(
        spec_imag, sin_fast, precision=highest
    )
    back_imag = jnp.matmul(spec_imag, cos_fast, precision=highest) + jnp.matmul(
        spec_real, sin_fast, precision=highest
    )
    cols_real, cols_imag = (
        lax.all_to_all(back_real, "ctx", split_axis=3, concat_axis=1, tiled=True),
        lax.all_to_all(back_imag, "ctx", split_axis=3, concat_axis=1, tiled=True),
    )
    turned_real = (cols_real * cos_twist - cols_imag * sin_twist).reshape(
        stacked, slow, channels * stride
    )
    turned_imag = (cols_imag * cos_twist + cols_real * sin_twist).reshape(
        stacked, slow, channels * stride
    )
    timeline = jnp.einsum("ka,skm->sam", cos_slow, turned_real, precision=highest) - jnp.einsum(
        "ka,skm->sam", sin_slow, turned_imag, precision=highest
    )
    timeline = timeline.reshape(stacked, devices, channels, stride)
    returned = lax.all_to_all(timeline, "ctx", split_axis=1, concat_axis=3, tiled=True)
    return returned[:, 0] / float(slow * fast)


def conv_product(gated_real, gated_imag, taps_real, taps_imag):
    conv_real = gated_real * taps_real - gated_imag * taps_imag
    conv_imag = gated_real * taps_imag + gated_imag * taps_real
    return (conv_real, conv_imag)


def corr_products(grad_real, grad_imag, gated_real, gated_imag, taps_real, taps_imag):
    corr_real = jnp.stack(
        [
            grad_real * taps_real + grad_imag * taps_imag,
            grad_real * gated_real + grad_imag * gated_imag,
        ]
    )
    corr_imag = jnp.stack(
        [
            grad_imag * taps_real - grad_real * taps_imag,
            grad_imag * gated_real - grad_real * gated_imag,
        ]
    )
    return (corr_real, corr_imag)


def by_residue(streams, filter_raw, grad_output):
    devices = lax.axis_size("ctx")
    position = lax.axis_index("ctx")
    channels, fast = filter_raw.shape
    slow = 2 * devices
    tap_scale = 1.0 / math.sqrt(fast * devices)
    tables = dft_tables(slow, fast, devices, position)
    query_part = streams[0].astype(jnp.float32)
    key_part = streams[1].astype(jnp.float32)
    value_part = streams[2].astype(jnp.float32)
    gated_input = key_part * value_part
    kernel_taps = filter_raw * tap_scale
    upstream = grad_output.astype(jnp.float32)
    grad_conv = query_part * upstream
    spec_real, spec_imag = forward_spectrum(jnp.stack([gated_input, kernel_taps]), tables)
    conv_real, conv_imag = conv_product(spec_real[0], spec_imag[0], spec_real[1], spec_imag[1])
    long_conv = inverse_signal(conv_real[None], conv_imag[None], tables)[0]
    grad_real, grad_imag = forward_spectrum(grad_conv[None], tables)
    corr_real, corr_imag = corr_products(
        grad_real[0], grad_imag[0], spec_real[0], spec_imag[0], spec_real[1], spec_imag[1]
    )
    both_back = inverse_signal(corr_real, corr_imag, tables)
    grad_gated = both_back[0]
    filter_back = both_back[1]
    grad_filter = filter_back * tap_scale
    mixed_out = (query_part * long_conv).astype(jnp.bfloat16)
    grad_query = (upstream * long_conv).astype(jnp.bfloat16)
    grad_key = (grad_gated * value_part).astype(jnp.bfloat16)
    grad_value = (grad_gated * key_part).astype(jnp.bfloat16)
    grad_streams = jnp.stack([grad_query, grad_key, grad_value], axis=0)
    return (mixed_out, grad_streams, grad_filter)


def table(angle):
    return np.cos(angle), np.sin(angle)


def circle(count, at):
    exact = {0: (1.0, 0.0), 1: (0.0, 1.0), 2: (-1.0, 0.0), 3: (0.0, -1.0)}
    at = at % count
    if 4 * at % count == 0:
        return exact[4 * at // count]
    return math.cos(2.0 * math.pi * at / count), math.sin(2.0 * math.pi * at / count)


def weighted(terms):
    total = None
    for weight, array in terms:
        if weight == 0.0 or array is None:
            continue
        if total is None:
            total = array if weight == 1.0 else -array if weight == -1.0 else array * weight
        elif weight == 1.0:
            total = total + array
        elif weight == -1.0:
            total = total - array
        else:
            total = total + array * weight
    return total


def transform_tables(block, fast, scale):
    slow = 2 * block
    length = slow * fast
    at = np.arange(fast)
    cos, sin = table(2.0 * np.pi / fast * (at[:, None] * at[None, :] % fast))
    matrix = np.block([[cos, -sin], [sin, cos]]).astype(np.float32)
    high = matrix.astype(jnp.bfloat16)
    low = (matrix - high.astype(np.float32)).astype(jnp.bfloat16)
    rows = np.arange(block + 1)
    cos, sin = table(2.0 * np.pi / length * (rows[:, None] * at[None, :] % length))
    weight = np.where((rows == 0) | (rows == block), 1.0, 2.0)[:, None] * scale / length
    turns = np.stack([np.concatenate([cos, sin]), np.concatenate([cos * weight, sin * weight])])
    return high, low, turns.astype(np.float32)


def by_partner(parts, place):
    parts = list(parts)
    step = 1
    while step < len(parts):
        crossed = (place & step) != 0
        parts = [jnp.where(crossed, parts[x ^ step], parts[x]) for x in range(len(parts))]
        step *= 2
    return parts


def product(left, high, low):
    left_high = left.astype(jnp.bfloat16)
    left_low = (left - left_high.astype(jnp.float32)).astype(jnp.bfloat16)

    def dot(a, b):
        return jnp.dot(a, b, preferred_element_type=jnp.float32)

    half = left.shape[0] // 2 // 16 * 16
    return jnp.concatenate(
        [
            dot(left_high[part], high) + (dot(left_low[part], high) + dot(left_high[part], low))
            for part in (slice(0, half), slice(half, left.shape[0]))
        ],
        axis=0,
    )


def exchange_order(devices):
    return [5, 1, 6, 0, 2, 4, 3, 7] if devices == 8 else list(range(devices))


def gate_kernel(streams_hbm, filter_hbm, upstream_hbm, out_ref, streams_ref, filter_ref, upstream_ref, arrived):
    devices, stacked, fast = out_ref.shape
    group = stacked // 3
    loads = [
        pltpu.make_async_copy(source, target, arrived.at[i])
        for i, (source, target) in enumerate(
            [(streams_hbm, streams_ref), (upstream_hbm, upstream_ref), (filter_hbm, filter_ref)]
        )
    ]
    for load in loads:
        load.start()
    for load in loads:
        load.wait()
    gated_input = streams_ref[1].astype(jnp.float32) * streams_ref[2].astype(jnp.float32)
    grad_conv = streams_ref[0].astype(jnp.float32) * upstream_ref[...].astype(jnp.float32)
    block = streams_ref.shape[1] // group
    for chunk, device in enumerate(exchange_order(devices)):
        share = slice(device % block * group, (device % block + 1) * group)
        out_ref[chunk, :group] = gated_input[share]
        out_ref[chunk, group : 2 * group] = filter_ref[share]
        out_ref[chunk, 2 * group :] = grad_conv[share]


def slow_transform(signal, slow):
    block = slow // 2
    real, imag = [None] * (block + 1), [None] * (block + 1)
    for k in range(block // 2 + 1):
        sums = [
            weighted([(circle(slow, a * k)[part], signal[a]) for a in range(parity, block, 2)])
            for part in range(2)
            for parity in range(2)
        ]
        cos_even, cos_odd, sin_even, sin_odd = sums
        real[k] = weighted([(1.0, cos_even), (1.0, cos_odd)])
        imag[k] = weighted([(-1.0, sin_even), (-1.0, sin_odd)])
        if 2 * k != block:
            real[block - k] = weighted([(1.0, cos_even), (-1.0, cos_odd)])
            imag[block - k] = weighted([(1.0, sin_even), (-1.0, sin_odd)])
    return real, imag


def slow_inverse(real, imag, slow):
    block = slow // 2
    half = block // 2
    results = [None] * block
    for parity in range(2):
        sign = 1.0 - 2.0 * parity
        cos_part = [weighted([(1.0, real[k]), (sign, real[block - k])]) for k in range(half)]
        sin_part = [weighted([(1.0, imag[k]), (-sign, imag[block - k])]) for k in range(half)]
        for a in range(parity, block, 2):
            terms = [(circle(slow, a * k)[0], cos_part[k]) for k in range(half)]
            terms += [(circle(slow, a * k)[1], sin_part[k]) for k in range(1, half)]
            terms += [(circle(slow, a * half)[0], real[half]), (circle(slow, a * half)[1], imag[half])]
            results[a] = weighted(terms)
    return results


def complex_sum(pairs):
    real, imag = None, None
    for first, second, conjugate in pairs:
        fast = first.shape[1] // 2
        (a, b), (c, d) = ((x[:, :fast], x[:, fast:]) for x in (first, second))
        one = a * c + b * d if conjugate else a * c - b * d
        two = b * c - a * d if conjugate else -(a * d + b * c)
        real, imag = (one, two) if real is None else (real + one, imag + two)
    return jnp.concatenate([real, imag], axis=1)


def convolve_kernel(signal_ref, high_ref, low_ref, turns_ref, *out_refs):
    devices, stacked, fast = signal_ref.shape
    group, block = stacked // 3, len(out_refs)
    slow, count = 2 * block, block + 1
    position = lax.axis_index("ctx")
    first_half = position < block

    def turn(which, k):
        return turns_ref[which, k : k + 1, :], turns_ref[which, count + k : count + k + 1, :]

    order = exchange_order(devices)
    signal = [signal_ref[order.index(a)] for a in range(devices)]
    halves = [slow_transform(signal[first : first + block], slow) for first in (0, block)]
    rows = []
    for k in range(count):
        cos, sin = turn(0, k)
        for real, imag in halves:
            if k == 0:
                turned = (real[k], jnp.zeros_like(real[k]))
            elif imag[k] is None:
                turned = (real[k] * cos, -(real[k] * sin))
            else:
                turned = (real[k] * cos + imag[k] * sin, imag[k] * cos - real[k] * sin)
            rows.append(jnp.concatenate(turned, axis=1))
    high, low = high_ref[...], low_ref[...]
    spectrum = product(jnp.concatenate(rows, axis=0), high, low)
    rows = []
    for k in range(count):
        parts = [spectrum[2 * k * stacked + i * group : 2 * k * stacked + (i + 1) * group] for i in range(6)]
        gated, taps, grad, gated_late, taps_late, grad_late = parts
        shift = 1.0 - 2.0 * (k % 2)
        nothing = jnp.zeros_like(gated)
        grad_near = jnp.where(first_half, weighted([(1.0, grad), (shift, grad_late)]), grad_late)
        grad_far = jnp.where(first_half, grad_late, nothing)
        gated_near = jnp.where(first_half, gated, weighted([(1.0, gated_late), (shift, gated)]))
        gated_far = jnp.where(first_half, nothing, gated)
        rows.append(complex_sum([(taps, gated_near, False), (taps_late, gated_far, False)]))
        rows.append(complex_sum([(taps, grad_near, True), (taps_late, grad_far, True)]))
        rows.append(complex_sum([(gated, grad_near, True), (gated_late, grad_far, True)]))
    back = product(jnp.concatenate(rows, axis=0), high, low)
    real, imag = [], []
    for k in range(count):
        cos, sin = turn(1, k)
        row = back[k * stacked : (k + 1) * stacked]
        real.append(row[:, :fast] * cos + row[:, fast:] * sin)
        imag.append(row[:, fast:] * cos - row[:, :fast] * sin)
    results = slow_inverse(real, imag, slow)
    for out_ref, result in zip(out_refs, by_partner(results, position % block), strict=True):
        out_ref[...] = result


def output_kernel(streams_ref, upstream_ref, *refs):
    back_refs, (mixed_ref, streams_grad_ref, filter_grad_ref) = refs[:-3], refs[-3:]
    channels, _ = filter_grad_ref.shape
    block = len(back_refs)
    group = channels // block
    parts = by_partner([back_refs[k][...] for k in [0, 2, 3, 1]], lax.axis_index("ctx") % block)
    long_conv = jnp.concatenate([part[:group] for part in parts], axis=0)
    grad_gated = jnp.concatenate([part[group : 2 * group] for part in parts], axis=0)
    filter_grad_ref[...] = jnp.concatenate([part[2 * group :] for part in parts], axis=0)
    mixed_ref[...] = (streams_ref[0].astype(jnp.float32) * long_conv).astype(jnp.bfloat16)
    streams_grad_ref[0] = (upstream_ref[...].astype(jnp.float32) * long_conv).astype(jnp.bfloat16)
    streams_grad_ref[1] = (streams_ref[2].astype(jnp.float32) * grad_gated).astype(jnp.bfloat16)
    streams_grad_ref[2] = (streams_ref[1].astype(jnp.float32) * grad_gated).astype(jnp.bfloat16)


def by_channel(streams, filter_raw, grad_output, block):
    devices = lax.axis_size("ctx")
    channels, fast = filter_raw.shape
    stacked = 3 * (channels // block)
    tap_scale = 1.0 / math.sqrt(fast * devices)
    vmem = pl.BlockSpec(memory_space=pltpu.VMEM)
    params = pltpu.CompilerParams(vmem_limit_bytes=8 << 20)
    signals = pl.pallas_call(
        gate_kernel,
        out_shape=jax.ShapeDtypeStruct((devices, stacked, fast), jnp.float32),
        in_specs=[pl.BlockSpec(memory_space=pltpu.HBM)] * 3,
        out_specs=vmem,
        scratch_shapes=[
            pltpu.VMEM(streams.shape, streams.dtype),
            pltpu.VMEM(filter_raw.shape, filter_raw.dtype),
            pltpu.VMEM(grad_output.shape, grad_output.dtype),
            pltpu.SemaphoreType.DMA((3,)),
        ],
        compiler_params=params,
    )(*(pltpu.with_memory_space_constraint(x, pltpu.HBM) for x in (streams, filter_raw, grad_output)))
    signals = lax.all_to_all(
        signals, "ctx", split_axis=0, concat_axis=0, axis_index_groups=[exchange_order(devices)], tiled=True
    )
    results = pl.pallas_call(
        convolve_kernel,
        out_shape=[jax.ShapeDtypeStruct((stacked, fast), jnp.float32)] * block,
        in_specs=[vmem] * 4,
        out_specs=[vmem] * block,
        compiler_params=params,
    )(signals, *transform_tables(block, fast, tap_scale))
    order = (3, 1, 2)
    results = list(results[:1]) + [lax.ppermute(results[x], "ctx", [(i, i ^ x) for i in range(devices)]) for x in order]
    return pl.pallas_call(
        output_kernel,
        out_shape=(
            jax.ShapeDtypeStruct((channels, fast), jnp.bfloat16),
            jax.ShapeDtypeStruct((3, channels, fast), jnp.bfloat16),
            jax.ShapeDtypeStruct((channels, fast), jnp.float32),
        ),
        in_specs=[vmem] * (2 + block),
        out_specs=(vmem,) * 3,
        compiler_params=params,
    )(streams, grad_output, *results)


def local(streams, filter_raw, grad_output):
    devices = lax.axis_size("ctx")
    channels, fast = filter_raw.shape
    block = 4
    if devices == 2 * block and channels % (16 * block) == 0 and fast % 128 == 0:
        return by_channel(streams, filter_raw, grad_output, block)
    return by_residue(streams, filter_raw, grad_output)


def solution(mesh):
    in_specs = (P(None, "tp", "ctx"), P("tp", "ctx"), P("tp", "ctx"))
    out_specs = (P("tp", "ctx"), P(None, "tp", "ctx"), P("tp", "ctx"))
    return jax.shard_map(local, mesh=mesh, in_specs=in_specs, out_specs=out_specs, check_vma=False)
```

```python
import math

import jax
import jax.numpy as jnp
import numpy as np
from jax import lax
from jax.experimental import pallas as pl
from jax.experimental.pallas import tpu as pltpu
from jax.sharding import PartitionSpec as P

highest = lax.Precision.HIGHEST


def dft_tables(slow, fast, devices, position):
    length = slow * fast
    stride = fast // devices
    freq_slow = jnp.arange(slow, dtype=jnp.int32)
    rows_slow = jnp.arange(devices, dtype=jnp.int32)
    angle_slow = (
        2.0 * math.pi / slow * (freq_slow[:, None] * rows_slow[None, :] % slow).astype(jnp.float32)
    )
    cols_twist = position * stride + jnp.arange(stride, dtype=jnp.int32)
    angle_twist = (
        2.0
        * math.pi
        / length
        * (freq_slow[:, None] * cols_twist[None, :] % length).astype(jnp.float32)
    )
    freq_fast = jnp.arange(fast, dtype=jnp.int32)
    angle_fast = (
        2.0 * math.pi / fast * (freq_fast[:, None] * freq_fast[None, :] % fast).astype(jnp.float32)
    )
    return (
        jnp.cos(angle_slow),
        jnp.sin(angle_slow),
        jnp.cos(angle_twist)[:, None, :],
        jnp.sin(angle_twist)[:, None, :],
        jnp.cos(angle_fast),
        jnp.sin(angle_fast),
    )


def forward_spectrum(signal, tables):
    cos_slow, sin_slow, cos_twist, sin_twist, cos_fast, sin_fast = tables
    stacked, channels, fast = signal.shape
    slow, devices = cos_slow.shape
    stride = fast // devices
    columns = lax.all_to_all(signal[:, None], "ctx", split_axis=3, concat_axis=1, tiled=True)
    flat = columns.reshape(stacked, devices, channels * stride)
    real_part = jnp.einsum("ka,sam->skm", cos_slow, flat, precision=highest).reshape(
        stacked, slow, channels, stride
    )
    imag_part = -jnp.einsum("ka,sam->skm", sin_slow, flat, precision=highest).reshape(
        stacked, slow, channels, stride
    )
    turned_real = real_part * cos_twist + imag_part * sin_twist
    turned_imag = imag_part * cos_twist - real_part * sin_twist
    rows_real, rows_imag = (
        lax.all_to_all(turned_real, "ctx", split_axis=1, concat_axis=3, tiled=True),
        lax.all_to_all(turned_imag, "ctx", split_axis=1, concat_axis=3, tiled=True),
    )
    spec_real = jnp.matmul(rows_real, cos_fast, precision=highest) + jnp.matmul(
        rows_imag, sin_fast, precision=highest
    )
    spec_imag = jnp.matmul(rows_imag, cos_fast, precision=highest) - jnp.matmul(
        rows_real, sin_fast, precision=highest
    )
    return (spec_real, spec_imag)


def inverse_signal(spec_real, spec_imag, tables):
    cos_slow, sin_slow, cos_twist, sin_twist, cos_fast, sin_fast = tables
    stacked, local_rows, channels, fast = spec_real.shape
    slow, devices = cos_slow.shape
    stride = fast // devices
    back_real = jnp.matmul(spec_real, cos_fast, precision=highest) - jnp.matmul(
        spec_imag, sin_fast, precision=highest
    )
    back_imag = jnp.matmul(spec_imag, cos_fast, precision=highest) + jnp.matmul(
        spec_real, sin_fast, precision=highest
    )
    cols_real, cols_imag = (
        lax.all_to_all(back_real, "ctx", split_axis=3, concat_axis=1, tiled=True),
        lax.all_to_all(back_imag, "ctx", split_axis=3, concat_axis=1, tiled=True),
    )
    turned_real = (cols_real * cos_twist - cols_imag * sin_twist).reshape(
        stacked, slow, channels * stride
    )
    turned_imag = (cols_imag * cos_twist + cols_real * sin_twist).reshape(
        stacked, slow, channels * stride
    )
    timeline = jnp.einsum("ka,skm->sam", cos_slow, turned_real, precision=highest) - jnp.einsum(
        "ka,skm->sam", sin_slow, turned_imag, precision=highest
    )
    timeline = timeline.reshape(stacked, devices, channels, stride)
    returned = lax.all_to_all(timeline, "ctx", split_axis=1, concat_axis=3, tiled=True)
    return returned[:, 0] / float(slow * fast)


def conv_product(gated_real, gated_imag, taps_real, taps_imag):
    conv_real = gated_real * taps_real - gated_imag * taps_imag
    conv_imag = gated_real * taps_imag + gated_imag * taps_real
    return (conv_real, conv_imag)


def corr_products(grad_real, grad_imag, gated_real, gated_imag, taps_real, taps_imag):
    corr_real = jnp.stack(
        [
            grad_real * taps_real + grad_imag * taps_imag,
            grad_real * gated_real + grad_imag * gated_imag,
        ]
    )
    corr_imag = jnp.stack(
        [
            grad_imag * taps_real - grad_real * taps_imag,
            grad_imag * gated_real - grad_real * gated_imag,
        ]
    )
    return (corr_real, corr_imag)


def by_residue(streams, filter_raw, grad_output):
    devices = lax.axis_size("ctx")
    position = lax.axis_index("ctx")
    channels, fast = filter_raw.shape
    slow = 2 * devices
    tap_scale = 1.0 / math.sqrt(fast * devices)
    tables = dft_tables(slow, fast, devices, position)
    query_part = streams[0].astype(jnp.float32)
    key_part = streams[1].astype(jnp.float32)
    value_part = streams[2].astype(jnp.float32)
    gated_input = key_part * value_part
    kernel_taps = filter_raw * tap_scale
    upstream = grad_output.astype(jnp.float32)
    grad_conv = query_part * upstream
    spec_real, spec_imag = forward_spectrum(jnp.stack([gated_input, kernel_taps]), tables)
    conv_real, conv_imag = conv_product(spec_real[0], spec_imag[0], spec_real[1], spec_imag[1])
    long_conv = inverse_signal(conv_real[None], conv_imag[None], tables)[0]
    grad_real, grad_imag = forward_spectrum(grad_conv[None], tables)
    corr_real, corr_imag = corr_products(
        grad_real[0], grad_imag[0], spec_real[0], spec_imag[0], spec_real[1], spec_imag[1]
    )
    both_back = inverse_signal(corr_real, corr_imag, tables)
    grad_gated = both_back[0]
    filter_back = both_back[1]
    grad_filter = filter_back * tap_scale
    mixed_out = (query_part * long_conv).astype(jnp.bfloat16)
    grad_query = (upstream * long_conv).astype(jnp.bfloat16)
    grad_key = (grad_gated * value_part).astype(jnp.bfloat16)
    grad_value = (grad_gated * key_part).astype(jnp.bfloat16)
    grad_streams = jnp.stack([grad_query, grad_key, grad_value], axis=0)
    return (mixed_out, grad_streams, grad_filter)


def table(angle):
    return np.cos(angle), np.sin(angle)


def circle(count, at):
    exact = {0: (1.0, 0.0), 1: (0.0, 1.0), 2: (-1.0, 0.0), 3: (0.0, -1.0)}
    at = at % count
    if 4 * at % count == 0:
        return exact[4 * at // count]
    return math.cos(2.0 * math.pi * at / count), math.sin(2.0 * math.pi * at / count)


def weighted(terms):
    total = None
    for weight, array in terms:
        if weight == 0.0 or array is None:
            continue
        if total is None:
            total = array if weight == 1.0 else -array if weight == -1.0 else array * weight
        elif weight == 1.0:
            total = total + array
        elif weight == -1.0:
            total = total - array
        else:
            total = total + array * weight
    return total


def transform_tables(block, fast, scale):
    slow = 2 * block
    length = slow * fast
    at = np.arange(fast)
    cos, sin = table(2.0 * np.pi / fast * (at[:, None] * at[None, :] % fast))
    matrix = np.block([[cos, -sin], [sin, cos]]).astype(np.float32)
    high = matrix.astype(jnp.bfloat16)
    low = (matrix - high.astype(np.float32)).astype(jnp.bfloat16)
    rows = np.arange(block + 1)
    cos, sin = table(2.0 * np.pi / length * (rows[:, None] * at[None, :] % length))
    weight = np.where((rows == 0) | (rows == block), 1.0, 2.0)[:, None] * scale / length
    turns = np.stack([np.concatenate([cos, sin]), np.concatenate([cos * weight, sin * weight])])
    return high, low, turns.astype(np.float32)


def by_partner(parts, place):
    parts = list(parts)
    step = 1
    while step < len(parts):
        crossed = (place & step) != 0
        parts = [jnp.where(crossed, parts[x ^ step], parts[x]) for x in range(len(parts))]
        step *= 2
    return parts


def product(left, high, low):
    left_high = left.astype(jnp.bfloat16)
    left_low = (left - left_high.astype(jnp.float32)).astype(jnp.bfloat16)

    def dot(a, b):
        return jnp.dot(a, b, preferred_element_type=jnp.float32)

    half = left.shape[0] // 2 // 16 * 16
    return jnp.concatenate(
        [
            dot(left_high[part], high) + (dot(left_low[part], high) + dot(left_high[part], low))
            for part in (slice(0, half), slice(half, left.shape[0]))
        ],
        axis=0,
    )


def exchange_order(devices):
    return [5, 1, 6, 4, 2, 0, 7, 3] if devices == 8 else list(range(devices))


def gate_kernel(streams_hbm, filter_hbm, upstream_hbm, out_ref, streams_ref, filter_ref, upstream_ref, arrived):
    devices, stacked, fast = out_ref.shape
    group = stacked // 3
    loads = [
        pltpu.make_async_copy(source, target, arrived.at[i])
        for i, (source, target) in enumerate(
            [(streams_hbm, streams_ref), (upstream_hbm, upstream_ref), (filter_hbm, filter_ref)]
        )
    ]
    for load in loads:
        load.start()
    for load in loads:
        load.wait()
    gated_input = streams_ref[1].astype(jnp.float32) * streams_ref[2].astype(jnp.float32)
    grad_conv = streams_ref[0].astype(jnp.float32) * upstream_ref[...].astype(jnp.float32)
    block = streams_ref.shape[1] // group
    for chunk, device in enumerate(exchange_order(devices)):
        share = slice(device % block * group, (device % block + 1) * group)
        out_ref[chunk, :group] = gated_input[share]
        out_ref[chunk, group : 2 * group] = filter_ref[share]
        out_ref[chunk, 2 * group :] = grad_conv[share]


def slow_transform(signal, slow):
    block = slow // 2
    real, imag = [None] * (block + 1), [None] * (block + 1)
    for k in range(block // 2 + 1):
        sums = [
            weighted([(circle(slow, a * k)[part], signal[a]) for a in range(parity, block, 2)])
            for part in range(2)
            for parity in range(2)
        ]
        cos_even, cos_odd, sin_even, sin_odd = sums
        real[k] = weighted([(1.0, cos_even), (1.0, cos_odd)])
        imag[k] = weighted([(-1.0, sin_even), (-1.0, sin_odd)])
        if 2 * k != block:
            real[block - k] = weighted([(1.0, cos_even), (-1.0, cos_odd)])
            imag[block - k] = weighted([(1.0, sin_even), (-1.0, sin_odd)])
    return real, imag


def slow_inverse(real, imag, slow):
    block = slow // 2
    half = block // 2
    results = [None] * block
    for parity in range(2):
        sign = 1.0 - 2.0 * parity
        cos_part = [weighted([(1.0, real[k]), (sign, real[block - k])]) for k in range(half)]
        sin_part = [weighted([(1.0, imag[k]), (-sign, imag[block - k])]) for k in range(half)]
        for a in range(parity, block, 2):
            terms = [(circle(slow, a * k)[0], cos_part[k]) for k in range(half)]
            terms += [(circle(slow, a * k)[1], sin_part[k]) for k in range(1, half)]
            terms += [(circle(slow, a * half)[0], real[half]), (circle(slow, a * half)[1], imag[half])]
            results[a] = weighted(terms)
    return results


def complex_sum(pairs):
    real, imag = None, None
    for first, second, conjugate in pairs:
        fast = first.shape[1] // 2
        (a, b), (c, d) = ((x[:, :fast], x[:, fast:]) for x in (first, second))
        one = a * c + b * d if conjugate else a * c - b * d
        two = b * c - a * d if conjugate else -(a * d + b * c)
        real, imag = (one, two) if real is None else (real + one, imag + two)
    return jnp.concatenate([real, imag], axis=1)


def convolve_kernel(signal_ref, high_ref, low_ref, turns_ref, *out_refs):
    devices, stacked, fast = signal_ref.shape
    group, block = stacked // 3, len(out_refs)
    slow, count = 2 * block, block + 1
    position = lax.axis_index("ctx")
    first_half = position < block

    def turn(which, k):
        return turns_ref[which, k : k + 1, :], turns_ref[which, count + k : count + k + 1, :]

    order = exchange_order(devices)
    signal = [signal_ref[order.index(a)] for a in range(devices)]
    halves = [slow_transform(signal[first : first + block], slow) for first in (0, block)]
    rows = []
    for k in range(count):
        cos, sin = turn(0, k)
        for real, imag in halves:
            if k == 0:
                turned = (real[k], jnp.zeros_like(real[k]))
            elif imag[k] is None:
                turned = (real[k] * cos, -(real[k] * sin))
            else:
                turned = (real[k] * cos + imag[k] * sin, imag[k] * cos - real[k] * sin)
            rows.append(jnp.concatenate(turned, axis=1))
    high, low = high_ref[...], low_ref[...]
    spectrum = product(jnp.concatenate(rows, axis=0), high, low)
    rows = []
    for k in range(count):
        parts = [spectrum[2 * k * stacked + i * group : 2 * k * stacked + (i + 1) * group] for i in range(6)]
        gated, taps, grad, gated_late, taps_late, grad_late = parts
        shift = 1.0 - 2.0 * (k % 2)
        nothing = jnp.zeros_like(gated)
        grad_near = jnp.where(first_half, weighted([(1.0, grad), (shift, grad_late)]), grad_late)
        grad_far = jnp.where(first_half, grad_late, nothing)
        gated_near = jnp.where(first_half, gated, weighted([(1.0, gated_late), (shift, gated)]))
        gated_far = jnp.where(first_half, nothing, gated)
        rows.append(complex_sum([(taps, gated_near, False), (taps_late, gated_far, False)]))
        rows.append(complex_sum([(taps, grad_near, True), (taps_late, grad_far, True)]))
        rows.append(complex_sum([(gated, grad_near, True), (gated_late, grad_far, True)]))
    back = product(jnp.concatenate(rows, axis=0), high, low)
    real, imag = [], []
    for k in range(count):
        cos, sin = turn(1, k)
        row = back[k * stacked : (k + 1) * stacked]
        real.append(row[:, :fast] * cos + row[:, fast:] * sin)
        imag.append(row[:, fast:] * cos - row[:, :fast] * sin)
    results = slow_inverse(real, imag, slow)
    for out_ref, result in zip(out_refs, by_partner(results, position % block), strict=True):
        out_ref[...] = result


def output_kernel(streams_ref, upstream_ref, *refs):
    back_refs, (mixed_ref, streams_grad_ref, filter_grad_ref) = refs[:-3], refs[-3:]
    channels, _ = filter_grad_ref.shape
    block = len(back_refs)
    group = channels // block
    parts = by_partner([back_refs[k][...] for k in [0, 3, 2, 1]], lax.axis_index("ctx") % block)
    long_conv = jnp.concatenate([part[:group] for part in parts], axis=0)
    grad_gated = jnp.concatenate([part[group : 2 * group] for part in parts], axis=0)
    filter_grad_ref[...] = jnp.concatenate([part[2 * group :] for part in parts], axis=0)
    mixed_ref[...] = (streams_ref[0].astype(jnp.float32) * long_conv).astype(jnp.bfloat16)
    streams_grad_ref[0] = (upstream_ref[...].astype(jnp.float32) * long_conv).astype(jnp.bfloat16)
    streams_grad_ref[1] = (streams_ref[2].astype(jnp.float32) * grad_gated).astype(jnp.bfloat16)
    streams_grad_ref[2] = (streams_ref[1].astype(jnp.float32) * grad_gated).astype(jnp.bfloat16)


def by_channel(streams, filter_raw, grad_output, block):
    devices = lax.axis_size("ctx")
    channels, fast = filter_raw.shape
    stacked = 3 * (channels // block)
    tap_scale = 1.0 / math.sqrt(fast * devices)
    vmem = pl.BlockSpec(memory_space=pltpu.VMEM)
    params = pltpu.CompilerParams(vmem_limit_bytes=8 << 20)
    signals = pl.pallas_call(
        gate_kernel,
        out_shape=jax.ShapeDtypeStruct((devices, stacked, fast), jnp.float32),
        in_specs=[pl.BlockSpec(memory_space=pltpu.HBM)] * 3,
        out_specs=vmem,
        scratch_shapes=[
            pltpu.VMEM(streams.shape, streams.dtype),
            pltpu.VMEM(filter_raw.shape, filter_raw.dtype),
            pltpu.VMEM(grad_output.shape, grad_output.dtype),
            pltpu.SemaphoreType.DMA((3,)),
        ],
        compiler_params=params,
    )(*(pltpu.with_memory_space_constraint(x, pltpu.HBM) for x in (streams, filter_raw, grad_output)))
    signals = lax.all_to_all(
        signals, "ctx", split_axis=0, concat_axis=0, axis_index_groups=[exchange_order(devices)], tiled=True
    )
    results = pl.pallas_call(
        convolve_kernel,
        out_shape=[jax.ShapeDtypeStruct((stacked, fast), jnp.float32)] * block,
        in_specs=[vmem] * 4,
        out_specs=[vmem] * block,
        compiler_params=params,
    )(signals, *transform_tables(block, fast, tap_scale))
    order = (3, 2, 1)
    results = list(results[:1]) + [lax.ppermute(results[x], "ctx", [(i, i ^ x) for i in range(devices)]) for x in order]
    return pl.pallas_call(
        output_kernel,
        out_shape=(
            jax.ShapeDtypeStruct((channels, fast), jnp.bfloat16),
            jax.ShapeDtypeStruct((3, channels, fast), jnp.bfloat16),
            jax.ShapeDtypeStruct((channels, fast), jnp.float32),
        ),
        in_specs=[vmem] * (2 + block),
        out_specs=(vmem,) * 3,
        compiler_params=params,
    )(streams, grad_output, *results)


def local(streams, filter_raw, grad_output):
    devices = lax.axis_size("ctx")
    channels, fast = filter_raw.shape
    block = 4
    if devices == 2 * block and channels % (16 * block) == 0 and fast % 128 == 0:
        return by_channel(streams, filter_raw, grad_output, block)
    return by_residue(streams, filter_raw, grad_output)


def solution(mesh):
    in_specs = (P(None, "tp", "ctx"), P("tp", "ctx"), P("tp", "ctx"))
    out_specs = (P("tp", "ctx"), P(None, "tp", "ctx"), P("tp", "ctx"))
    return jax.shard_map(local, mesh=mesh, in_specs=in_specs, out_specs=out_specs, check_vma=False)
```
